512 devices in a mesh: row: 32 (over y, x), col: 16 (over z, core).
Axes of the slice: x: 4, y: 8, z: 8, core: 2. Of those that a mesh axis runs over, the one named last changes fastest.
Arguments:
- source_features: bfloat16 [16, 2048, 256], P('col', 'row'), may hold values from -500 to 500
- target_features: bfloat16 [32768, 256], P(('row', 'col')), may hold values from -6 to 6
- weight: bfloat16 [256, 256], replicated, may hold values from -0.375 to 0.375
- score_source: float32 [4, 64], replicated, may hold values from -0.75 to 0.75
- score_target: float32 [4, 64], replicated, may hold values from -0.75 to 0.75
- out_bias: float32 [256], replicated, may hold values from -3 to 3
- block_list: int32 [32, 16, 48], P('row', 'col'), may hold values from 0 to 127, as said below
- block_count: int32 [32, 16], P('row', 'col'), may hold values from 8 to 48, as said below
- edge_bits: int32 [32, 16, 48, 16, 128], P('row', 'col'), may hold values from 0 to 255, as said below
Outputs:
- updated: bfloat16 [32768, 256], P(('row', 'col'))
The draws below stay inside these ranges and needn't reach their ends.
Inputs may be any that keep to these rules, and one draw needn't show every extreme that they name: `block_list`: slot s of tile (r, c) names target block p // 16 and source block p % 16 of the tile; the first block_count[r, c] slots of a tile name distinct blocks and later slots are unused. `block_count`: some tile holds 48 blocks. `edge_bits`: bit b of entry [r, c, s, w, i] marks the edge from source 8 w + b to target i of the block in slot s. Some targets have no edge.
All inputs are finite; a program needn't handle non-finite values.
Results may differ from the reference program's by a relative error of at most 0.007.
The reference program's roundings to bfloat16 on the way (of `projected` and `weights`) count: a program that leaves them out, or rounds other values in their place, can miss the bound.
Values may be sent and summed in bfloat16 or wider, within the bound.
A program may use at most 64 MiB of HBM per device.

```python
import jax
import jax.numpy as jnp
from jax import lax

D = 256
H = 4
HD = 64
BLK = 128
DB = 8
SB = 16
MAXB = 48
NSRC = 32768
NDST = 32768
N_ROW = 32
N_COL = 16


def graph_tables(key):
    base = jax.random.fold_in(key, 7)
    key_count, key_full, key_perm, key_bits, key_empty = jax.random.split(base, 5)
    tiles = N_ROW * N_COL
    lowest = max(1, MAXB // 6)
    counts = jax.random.randint(key_count, (tiles,), lowest, MAXB + 1).astype(jnp.int32)
    chosen = jax.random.randint(key_full, (), 0, tiles)
    counts = jnp.where(jnp.arange(tiles) == chosen, MAXB, counts).astype(jnp.int32)
    perm_keys = jax.random.split(key_perm, tiles)
    slots = jax.vmap(lambda one: jax.random.permutation(one, DB * SB)[:MAXB])(perm_keys).astype(jnp.int32)
    packed = jnp.zeros((tiles, MAXB, BLK // 8, BLK), jnp.int32)
    for bit in range(8):
        setting = jax.random.randint(jax.random.fold_in(key_bits, bit), (tiles, MAXB, BLK // 8, BLK), 0, 20) == 0
        packed = packed + jnp.where(setting, 1 << bit, 0).astype(jnp.int32)
    empty = jax.random.randint(key_empty, (N_ROW, DB * BLK), 0, 40) == 0
    tile_row = jnp.arange(tiles) // N_COL
    target = (slots // SB)[:, :, None] * BLK + jnp.arange(BLK)[None, None, :]
    blank = empty[tile_row[:, None, None], target]
    packed = jnp.where(blank[:, :, None, :], 0, packed).astype(jnp.int32)
    return (slots.reshape(N_ROW, N_COL, MAXB), counts.reshape(N_ROW, N_COL), packed.reshape(N_ROW, N_COL, MAXB, BLK // 8, BLK))


def draw_block_list(key, part):
    return graph_tables(key)[0]


def draw_block_count(key, part):
    return graph_tables(key)[1]


def draw_edge_bits(key, part):
    return graph_tables(key)[2]


def draw_source_features(key, part):
    key_base = jax.random.fold_in(jax.random.fold_in(key, 11), 0)
    shape = (N_COL, SB * BLK, D)
    values = jnp.clip(jax.random.normal(key_base, shape, jnp.float32), -8.0, 8.0)
    return values.astype(jnp.bfloat16)


def steps_of(key, dims, cuts, smallest, high):
    gain, own = 1.0, jax.random.fold_in(key, 6)
    for axis_at, shards_of in cuts:
        heights = jnp.exp(jax.random.uniform(jax.random.fold_in(own, axis_at), (shards_of,), jnp.float32, smallest / len(cuts), high / len(cuts)))
        gain = gain * jnp.repeat(heights, dims[axis_at] // shards_of).reshape([-1 if axis == axis_at else 1 for axis in range(len(dims))])
    return gain


def noise(own_key, shape, scale, reach, shards=(), kind=jnp.bfloat16):
    values = scale * jax.random.normal(own_key, shape, jnp.float32)
    if shards:
        values = values * steps_of(own_key, shape, shards, -0.22, 0.18)
    return jnp.clip(values, -reach, reach).astype(kind)


def setup_inputs(seed: int = 0) -> dict:
    seeds = jax.random.split(jax.random.key(seed), 10)
    return {
        "source_features": draw_source_features(jax.random.fold_in(seeds[9], 71), 0),
        "target_features": noise(seeds[1], (NDST, D), 1.0, 6.0, ((0, 512),)),
        "weight": noise(seeds[2], (D, H * HD), D ** -0.5, 0.375),
        "score_source": noise(seeds[3], (H, HD), HD ** -0.5, 0.75, (), jnp.float32),
        "score_target": noise(seeds[4], (H, HD), HD ** -0.5, 0.75, (), jnp.float32),
        "out_bias": noise(seeds[5], (H * HD,), 0.5, 3.0, (), jnp.float32),
        "block_list": draw_block_list(jax.random.fold_in(seeds[9], 71), 0),
        "block_count": draw_block_count(jax.random.fold_in(seeds[9], 71), 0),
        "edge_bits": draw_edge_bits(jax.random.fold_in(seeds[9], 71), 0),
    }


very_low = -1e30
slope = 0.2
per_step = 4


def unpack(packed):
    shifts = jnp.arange(8, dtype=jnp.int32)
    spread = jnp.right_shift(packed[:, None, :], shifts[None, :, None]) & 1
    return spread.reshape(packed.shape[0] * 8, packed.shape[1]) > 0


def block_scores(src_logits, dst_logits, position):
    dst_block = (position // SB).astype(jnp.int32)
    src_block = (position % SB).astype(jnp.int32)
    zero = jnp.zeros((), jnp.int32)
    head_count = src_logits.shape[0]
    from_src = lax.dynamic_slice(src_logits, (zero, src_block * BLK), (head_count, BLK))
    from_dst = lax.dynamic_slice(dst_logits, (zero, dst_block * BLK), (head_count, BLK))
    raw = from_src[:, :, None] + from_dst[:, None, :]
    return dst_block, src_block, jnp.where(raw > 0, raw, slope * raw)


def tile_max(src_logits, dst_logits, slots, live, packed, row_max):
    zero = jnp.zeros((), jnp.int32)
    head_count = src_logits.shape[0]

    def advance(group, row_max):
        first = jnp.asarray(group, jnp.int32) * per_step
        for member in range(per_step):
            slot = first + member
            edge_mask = unpack(packed[slot]) & (slot < live)
            dst_block, src_block, scores = block_scores(src_logits, dst_logits, slots[slot])
            block_max = jnp.max(jnp.where(edge_mask[None], scores, very_low), axis=1)
            prior = lax.dynamic_slice(row_max, (zero, dst_block * BLK), (head_count, BLK))
            row_max = lax.dynamic_update_slice(row_max, jnp.maximum(prior, block_max), (zero, dst_block * BLK))
        return row_max

    return lax.fori_loop(0, slots.shape[0] // per_step, advance, row_max)


def tile_sum(features, src_logits, dst_logits, slots, live, packed, row_max, carry):
    zero = jnp.zeros((), jnp.int32)
    head_count = src_logits.shape[0]
    out_width = features.shape[1]
    head_size = out_width // head_count

    def advance(group, carry):
        accum, denoms = carry
        first = jnp.asarray(group, jnp.int32) * per_step
        for member in range(per_step):
            slot = first + member
            edge_mask = unpack(packed[slot]) & (slot < live)
            dst_block, src_block, scores = block_scores(src_logits, dst_logits, slots[slot])
            prior_max = lax.dynamic_slice(row_max, (zero, dst_block * BLK), (head_count, BLK))
            numer = jnp.exp(jnp.where(edge_mask[None], scores - prior_max[:, None, :], very_low))
            old_denoms = lax.dynamic_slice(denoms, (dst_block * BLK, zero), (BLK, head_count))
            denoms = lax.dynamic_update_slice(denoms, old_denoms + jnp.sum(numer, axis=1).T, (dst_block * BLK, zero))
            weights = numer.astype(jnp.bfloat16)
            src_feats = lax.dynamic_slice(features, (src_block * BLK, zero), (BLK, out_width)).reshape(BLK, head_count, head_size)
            product = jnp.einsum("hji,jhk->ihk", weights.astype(jnp.float32), src_feats.astype(jnp.float32), precision=lax.Precision.HIGHEST).reshape(BLK, out_width)
            old_accum = lax.dynamic_slice(accum, (dst_block * BLK, zero), (BLK, out_width))
            accum = lax.dynamic_update_slice(accum, old_accum + product, (dst_block * BLK, zero))
        return accum, denoms

    return lax.fori_loop(0, slots.shape[0] // per_step, advance, carry)


def reference(source_features, target_features, weight, score_source, score_target, out_bias, block_list, block_count, edge_bits):
    head_count = H
    out_width = H * HD
    src_rows = SB * BLK
    dst_rows = DB * BLK
    zero = jnp.zeros((), jnp.int32)
    projected = jnp.dot(source_features.reshape(NSRC, D), weight, preferred_element_type=jnp.float32).astype(jnp.bfloat16)
    src_all = jnp.einsum("nhk,hk->hn", projected.reshape(NSRC, H, HD).astype(jnp.float32), score_source, precision=lax.Precision.HIGHEST)
    dst_proj = jnp.dot(target_features, weight, preferred_element_type=jnp.float32)
    dst_all = jnp.einsum("nhk,hk->hn", dst_proj.reshape(NDST, H, HD), score_target, precision=lax.Precision.HIGHEST)

    def row_block(index):
        index = index.astype(jnp.int32)
        dst_logits = lax.dynamic_slice(dst_all, (zero, index * dst_rows), (head_count, dst_rows))

        def column_max(column, row_max):
            column = jnp.asarray(column, jnp.int32)
            src_logits = lax.dynamic_slice(src_all, (zero, column * src_rows), (head_count, src_rows))
            return tile_max(src_logits, dst_logits, block_list[index, column], block_count[index, column], edge_bits[index, column], row_max)

        row_max = lax.fori_loop(0, N_COL, column_max, jnp.full((head_count, dst_rows), very_low, jnp.float32))

        def column_sum(column, carry):
            column = jnp.asarray(column, jnp.int32)
            src_logits = lax.dynamic_slice(src_all, (zero, column * src_rows), (head_count, src_rows))
            features = lax.dynamic_slice(projected, (column * src_rows, zero), (src_rows, out_width))
            return tile_sum(features, src_logits, dst_logits, block_list[index, column], block_count[index, column], edge_bits[index, column], row_max, carry)

        start = (jnp.zeros((dst_rows, out_width), jnp.float32), jnp.zeros((dst_rows, head_count), jnp.float32))
        accum, denoms = lax.fori_loop(0, N_COL, column_sum, start)
        blended = accum.reshape(dst_rows, head_count, HD) / jnp.maximum(denoms, 1.0)[:, :, None]
        return jax.nn.elu(blended.reshape(dst_rows, out_width) + out_bias).astype(jnp.bfloat16)

    stacked = lax.map(row_block, jnp.arange(N_ROW, dtype=jnp.int32))
    return stacked.reshape(NDST, out_width)
```

```python
import functools

import jax
import jax.numpy as jnp
from jax import lax
from jax.experimental import pallas as pl
from jax.experimental.pallas import tpu as pltpu
from jax.sharding import PartitionSpec as P

BLK = 128
SB = 16
DB = 8
HEADS = 4
HD = 64
WIDTH = 256
ROWS = 32
COLS = 16
OWN = 64

very_low = -1e30
no_edge = -3e38
slope = 0.2
MESH = pl.DeviceIdType.MESH
by_columns = (((1,), (1,)), ((), ()))


def in_three(x):
    high = x.astype(jnp.bfloat16)
    rest = x - high.astype(jnp.float32)
    middle = rest.astype(jnp.bfloat16)
    low = (rest - middle.astype(jnp.float32)).astype(jnp.bfloat16)
    return high, middle, low


def leaky(x):
    return jnp.maximum(x, slope * x)


def gather_kernel(
    src_ref, tgt_ref, weight_ref, target_ref, feats_ref, logits_ref,
    own_ref, own_logits, send_a, recv_a, send_b, recv_b,
):
    row, col = lax.axis_index("row"), lax.axis_index("col")
    barrier = pltpu.get_barrier_semaphore()

    def greet_row(d, _):
        pl.semaphore_signal(barrier, inc=1, device_id=(lax.rem(row + d, ROWS), col), device_id_type=MESH)
        return 0

    def greet_col(d, _):
        pl.semaphore_signal(barrier, inc=1, device_id=(row, lax.rem(col + d, COLS)), device_id_type=MESH)
        return 0

    lax.fori_loop(1, ROWS, greet_row, 0)
    lax.fori_loop(1, COLS, greet_col, 0)
    own = jnp.dot(src_ref[...], weight_ref[...], preferred_element_type=jnp.float32)
    own_ref[...] = own.astype(jnp.bfloat16)
    product = jnp.dot(tgt_ref[...], weight_ref[...], preferred_element_type=jnp.float32) * target_ref[...]
    head_of = lax.broadcasted_iota(jnp.int32, (8, WIDTH), 1) // HD
    pick = (head_of == lax.broadcasted_iota(jnp.int32, (8, WIDTH), 0)).astype(jnp.bfloat16)
    high, middle, low = in_three(product)
    logits = lax.dot_general(pick, low, by_columns, preferred_element_type=jnp.float32)
    logits += lax.dot_general(pick, middle, by_columns, preferred_element_type=jnp.float32)
    logits += lax.dot_general(pick, high, by_columns, preferred_element_type=jnp.float32)
    twice = jnp.concatenate([logits, logits], axis=1)
    half = lax.broadcasted_iota(jnp.int32, (8, BLK), 1) // OWN
    own_logits[...] = jnp.where(half == lax.rem(col, 2), twice, 0.0)
    feats_ref[row] = own_ref[...]
    logits_ref[col] = own_logits[...]
    pl.semaphore_wait(barrier, ROWS + COLS - 2)

    def logits_copy(d):
        return pltpu.make_async_remote_copy(
            src_ref=own_logits, dst_ref=logits_ref.at[col], send_sem=send_b.at[d], recv_sem=recv_b.at[d],
            device_id=(row, lax.rem(col + d, COLS)), device_id_type=MESH,
        )

    def feats_copy(d):
        return pltpu.make_async_remote_copy(
            src_ref=own_ref, dst_ref=feats_ref.at[row], send_sem=send_a.at[d], recv_sem=recv_a.at[d],
            device_id=(lax.rem(row + d, ROWS), col), device_id_type=MESH,
        )

    def start_logits(d, _):
        logits_copy(d).start()
        return 0

    def start_feats(d, _):
        feats_copy(d).start()
        return 0

    def wait_logits(d, _):
        logits_copy(d).wait()
        return 0

    def wait_feats(d, _):
        feats_copy(d).wait()
        return 0

    lax.fori_loop(1, COLS, start_logits, 0)
    lax.fori_loop(1, ROWS, start_feats, 0)
    lax.fori_loop(1, COLS, wait_logits, 0)
    lax.fori_loop(1, ROWS, wait_feats, 0)


def gather(source, target, weight, score_target):
    vmem = pl.BlockSpec(memory_space=pltpu.VMEM)
    return pl.pallas_call(
        gather_kernel,
        out_shape=(
            jax.ShapeDtypeStruct((ROWS, OWN, WIDTH), jnp.bfloat16),
            jax.ShapeDtypeStruct((COLS, 8, BLK), jnp.float32),
        ),
        in_specs=[vmem] * 4,
        out_specs=(vmem, vmem),
        scratch_shapes=[
            pltpu.VMEM((OWN, WIDTH), jnp.bfloat16),
            pltpu.VMEM((8, BLK), jnp.float32),
            pltpu.SemaphoreType.DMA((ROWS,)),
            pltpu.SemaphoreType.DMA((ROWS,)),
            pltpu.SemaphoreType.DMA((COLS,)),
            pltpu.SemaphoreType.DMA((COLS,)),
        ],
        compiler_params=pltpu.CompilerParams(collective_id=0, has_side_effects=True, vmem_limit_bytes=16 << 20),
        name="gather",
    )(source, target, weight, score_target)


def tile_kernel(
    slots_ref, live_ref, feats_ref, logits_ref, bits_ref, source_ref, sums_ref, maxima_ref,
    turned, spread, dst, best, total, accum, weights,
):
    live = live_ref[0]
    head_of = lax.broadcasted_iota(jnp.int32, (BLK, WIDTH), 1) // HD
    pick = head_of == lax.broadcasted_iota(jnp.int32, (BLK, WIDTH), 0)
    score = in_three(jnp.where(pick, source_ref[...], 0.0))
    eye = (lax.broadcasted_iota(jnp.int32, (WIDTH, WIDTH), 0) == lax.broadcasted_iota(jnp.int32, (WIDTH, WIDTH), 1)).astype(jnp.bfloat16)
    for d in range(DB):
        dst[d] = logits_ref[2 * d] + logits_ref[2 * d + 1]
    best[...] = jnp.full(best.shape, no_edge, jnp.float32)
    total[...] = jnp.zeros(total.shape, jnp.float32)
    accum[...] = jnp.zeros(accum.shape, jnp.float32)

    @pl.loop(0, SB)
    def _(s):
        rows = pl.ds(pl.multiple_of(s * BLK, BLK), BLK)
        block = feats_ref[rows, :]
        flipped = lax.dot_general(eye, block, by_columns, preferred_element_type=jnp.float32)
        turned[s] = flipped.astype(jnp.bfloat16)
        logits = lax.dot_general(block, score[2], by_columns, preferred_element_type=jnp.float32)
        logits += lax.dot_general(block, score[1], by_columns, preferred_element_type=jnp.float32)
        logits += lax.dot_general(block, score[0], by_columns, preferred_element_type=jnp.float32)
        for h in range(HEADS):
            spread[h, rows, :] = jnp.broadcast_to(logits[:, h : h + 1], (BLK, BLK))

    bit = jnp.left_shift(1, lax.broadcasted_iota(jnp.int32, (8, BLK), 0))

    def edges(slot, w):
        words = bits_ref[slot, pl.ds(w, 1), :]
        return (jnp.broadcast_to(words, (8, BLK)) & bit) != 0

    @pl.loop(0, live)
    def _(slot):
        place = slots_ref[slot]
        d, s = place // SB, lax.rem(place, SB)
        top = [best[d, h] for h in range(HEADS)]
        for w in range(BLK // 8):
            mask = edges(slot, w)
            rows = pl.ds(pl.multiple_of(s * BLK + 8 * w, 8), 8)
            for h in range(HEADS):
                top[h] = jnp.maximum(top[h], jnp.where(mask, spread[h, rows, :], no_edge))
        for h in range(HEADS):
            best[d, h] = top[h]

    maxima_ref[...] = jnp.zeros(maxima_ref.shape, jnp.float32)
    for d in range(DB):
        for h in range(HEADS):
            top = jnp.max(best[d, h], axis=0, keepdims=True)
            value = leaky(top + dst[d, h : h + 1, :])
            maxima_ref[d, h : h + 1, :] = jnp.where(top > -1e38, value, very_low)

    @pl.loop(0, live)
    def _(slot):
        place = slots_ref[slot]
        d, s = place // SB, lax.rem(place, SB)
        sums = [total[d, h] for h in range(HEADS)]
        b = [jnp.broadcast_to(dst[d, pl.ds(h, 1), :], (8, BLK)) for h in range(HEADS)]
        m = [jnp.broadcast_to(maxima_ref[d, pl.ds(h, 1), :], (8, BLK)) for h in range(HEADS)]
        for w in range(0, BLK // 8, 2):
            masks = [edges(slot, w), edges(slot, w + 1)]
            for h in range(HEADS):
                pair = []
                for half in range(2):
                    rows = pl.ds(pl.multiple_of(s * BLK + 8 * (w + half), 8), 8)
                    score = leaky(spread[h, rows, :] + b[h]) - m[h]
                    numer = jnp.where(masks[half], jnp.exp(score), 0.0)
                    sums[h] = sums[h] + numer
                    pair.append(numer)
                weights[h, 8 * w : 8 * w + 16, :] = jnp.concatenate(pair, axis=0).astype(jnp.bfloat16)
        for h in range(HEADS):
            total[d, h] = sums[h]
            part = jnp.dot(turned[s, h * HD : (h + 1) * HD, :], weights[h], preferred_element_type=jnp.float32)
            accum[d, h * HD : (h + 1) * HD, :] += part

    for d in range(DB):
        for h in range(HEADS):
            maxima_ref[d, HEADS + h : HEADS + h + 1, :] = jnp.sum(total[d, h], axis=0, keepdims=True)
        back = lax.dot_general(
            eye[:BLK, :BLK], accum[d].astype(jnp.bfloat16), by_columns, preferred_element_type=jnp.float32
        ).astype(jnp.bfloat16)
        sums_ref[2 * d] = back[:OWN]
        sums_ref[2 * d + 1] = back[OWN:]


def attend(slots, live, feats, logits, bits, score_source):
    vmem = pl.BlockSpec(memory_space=pltpu.VMEM)
    smem = pl.BlockSpec(memory_space=pltpu.SMEM)
    return pl.pallas_call(
        tile_kernel,
        out_shape=(
            jax.ShapeDtypeStruct((COLS, OWN, WIDTH), jnp.bfloat16),
            jax.ShapeDtypeStruct((DB, 8, BLK), jnp.float32),
        ),
        in_specs=[smem, smem, vmem, vmem, vmem, vmem],
        out_specs=(vmem, vmem),
        scratch_shapes=[
            pltpu.VMEM((SB, WIDTH, BLK), jnp.bfloat16),
            pltpu.VMEM((HEADS, SB * BLK, BLK), jnp.float32),
            pltpu.VMEM((DB, 8, BLK), jnp.float32),
            pltpu.VMEM((DB, HEADS, 8, BLK), jnp.float32),
            pltpu.VMEM((DB, HEADS, 8, BLK), jnp.float32),
            pltpu.VMEM((DB, WIDTH, BLK), jnp.float32),
            pltpu.VMEM((HEADS, BLK, BLK), jnp.bfloat16),
        ],
        compiler_params=pltpu.CompilerParams(vmem_limit_bytes=32 << 20),
        name="attend",
    )(slots, live, feats, logits, bits, score_source)


def combine_kernel(
    sums_ref, maxima_ref, bias_ref, out_ref, got_sums, got_max, send_a, recv_a, send_b, recv_b,
):
    row, col = lax.axis_index("row"), lax.axis_index("col")
    barrier = pltpu.get_barrier_semaphore()

    def greet(d, _):
        pl.semaphore_signal(barrier, inc=1, device_id=(row, lax.rem(col + d, COLS)), device_id_type=MESH)
        return 0

    lax.fori_loop(1, COLS, greet, 0)
    got_sums[col] = sums_ref[col]
    got_max[col] = maxima_ref[col // 2]
    pl.semaphore_wait(barrier, COLS - 1)

    def max_copy(d):
        peer = lax.rem(col + d, COLS)
        return pltpu.make_async_remote_copy(
            src_ref=maxima_ref.at[peer // 2], dst_ref=got_max.at[col], send_sem=send_b.at[d], recv_sem=recv_b.at[d],
            device_id=(row, peer), device_id_type=MESH,
        )

    def sums_copy(d):
        peer = lax.rem(col + d, COLS)
        return pltpu.make_async_remote_copy(
            src_ref=sums_ref.at[peer], dst_ref=got_sums.at[col], send_sem=send_a.at[d], recv_sem=recv_a.at[d],
            device_id=(row, peer), device_id_type=MESH,
        )

    def start_max(d, _):
        max_copy(d).start()
        return 0

    def start_sums(d, _):
        sums_copy(d).start()
        return 0

    def wait_max(d, _):
        max_copy(d).wait()
        return 0

    def wait_sums(d, _):
        sums_copy(d).wait()
        return 0

    lax.fori_loop(1, COLS, start_max, 0)
    lax.fori_loop(1, COLS, start_sums, 0)
    lax.fori_loop(1, COLS, wait_max, 0)
    every = got_max[...]
    local = every[:, :HEADS, :]
    top = jnp.max(local, axis=0, keepdims=True)
    factor = jnp.exp(local - top)
    denoms = jnp.sum(factor * every[:, HEADS:, :], axis=0, keepdims=True)
    factor = factor / jnp.maximum(denoms, 1.0)
    flat = jnp.concatenate([factor[c] for c in range(COLS)] + [jnp.zeros((BLK - COLS * HEADS, BLK), jnp.float32)], axis=0)
    turned = flat.T
    turned = jnp.where(lax.rem(col, 2) == 0, turned[:OWN], turned[OWN:])
    lax.fori_loop(1, COLS, wait_sums, 0)
    parts = [jnp.zeros((OWN, HD), jnp.float32)] * HEADS
    for c in range(COLS):
        for h in range(HEADS):
            scale = jnp.broadcast_to(turned[:, c * HEADS + h : c * HEADS + h + 1], (OWN, HD))
            parts[h] = parts[h] + scale * got_sums[c, :, h * HD : (h + 1) * HD].astype(jnp.float32)
    blended = jnp.concatenate(parts, axis=1) + bias_ref[...]
    result = jnp.where(blended > 0, blended, jnp.exp(jnp.minimum(blended, 0.0)) - 1.0)
    out_ref[...] = result.astype(jnp.bfloat16)


def combine(sums, maxima, bias):
    vmem = pl.BlockSpec(memory_space=pltpu.VMEM)
    return pl.pallas_call(
        combine_kernel,
        out_shape=jax.ShapeDtypeStruct((OWN, WIDTH), jnp.bfloat16),
        in_specs=[vmem] * 3,
        out_specs=vmem,
        scratch_shapes=[
            pltpu.VMEM((COLS, OWN, WIDTH), jnp.bfloat16),
            pltpu.VMEM((COLS, 8, BLK), jnp.float32),
            pltpu.SemaphoreType.DMA((COLS,)),
            pltpu.SemaphoreType.DMA((COLS,)),
            pltpu.SemaphoreType.DMA((COLS,)),
            pltpu.SemaphoreType.DMA((COLS,)),
        ],
        compiler_params=pltpu.CompilerParams(collective_id=1, has_side_effects=True, vmem_limit_bytes=16 << 20),
        name="combine",
    )(sums, maxima, bias)


def body(
    source_features, target_features, weight, score_source, score_target, out_bias,
    block_list, block_count, edge_bits,
):
    feats, logits = gather(source_features[0], target_features, weight, score_target.reshape(1, WIDTH))
    sums, maxima = attend(
        block_list[0, 0], block_count[0], feats.reshape(SB * BLK, WIDTH), logits, edge_bits[0, 0],
        score_source.reshape(1, WIDTH),
    )
    return combine(sums, maxima, out_bias.reshape(1, WIDTH))


def solution(mesh):
    placed = (
        P("col", "row", None),
        P(("row", "col"), None),
        P(),
        P(),
        P(),
        P(),
        P("row", "col", None),
        P("row", "col"),
        P("row", "col", None, None, None),
    )
    return jax.shard_map(
        body, mesh=mesh, in_specs=placed, out_specs=P(("row", "col"), None), check_vma=False
    )
```

```python
import jax
import jax.numpy as jnp
from jax import lax
from jax.experimental import pallas as pl
from jax.experimental.pallas import tpu as pltpu
from jax.sharding import PartitionSpec as P

BLK = 128
SB = 16
DB = 8
SLOTS = 48
HEADS = 4
HD = 64
WIDTH = 256
ROWS = 32
COLS = 16
XS = 4
YS = 8
ZS = 8
OWN = 64

very_low = -1e30
no_edge = -3e38
slope = 0.2
MESH = pl.DeviceIdType.MESH
by_columns = (((1,), (1,)), ((), ()))


def in_three(x):
    high = x.astype(jnp.bfloat16)
    rest = x - high.astype(jnp.float32)
    middle = rest.astype(jnp.bfloat16)
    low = (rest - middle.astype(jnp.float32)).astype(jnp.bfloat16)
    return low, middle, high


def leaky(x):
    return jnp.maximum(x, slope * x)


def loop(first, last, step):
    def one(i, _):
        step(i)
        return 0

    lax.fori_loop(first, last, one, 0)


def in_half(rows, position):
    twice = jnp.concatenate([rows, rows], axis=1)
    half = lax.broadcasted_iota(jnp.int32, (8, BLK), 1) // OWN
    return jnp.where(half == lax.rem(position, 2), twice, 0.0)


def flat_scores(ref):
    return jnp.concatenate([ref[h : h + 1, :] for h in range(HEADS)], axis=1)


def scores_kernel(
    src_hbm, tgt_hbm, weight_hbm, source_hbm, target_hbm, slots_hbm, live_hbm, bits_hbm,
    u_ref, v_ref, weights_ref, sums_ref, maxima_ref,
    src_ref, tgt_ref, weight_ref, source_ref, target_ref, slots_ref, live_ref, bits_ref,
    src_rows, dst_rows, spread, dst, tops, best,
    local, send_a, recv_a, send_b, recv_b, send_x, recv_x, send_y, recv_y,
    send_up, recv_up, send_down, recv_down, send_f, recv_f,
):
    row, col = lax.axis_index("row"), lax.axis_index("col")
    x, y = lax.rem(row, XS), row // XS
    pairs = (
        (weight_hbm, weight_ref), (src_hbm, src_ref), (tgt_hbm, tgt_ref), (source_hbm, source_ref),
        (target_hbm, target_ref), (slots_hbm, slots_ref), (live_hbm, live_ref), (bits_hbm, bits_ref),
    )
    loads = [pltpu.make_async_copy(a, b, local.at[i]) for i, (a, b) in enumerate(pairs)]
    for load in loads:
        load.start()
    barrier = pltpu.get_barrier_semaphore()

    def greet_row(d):
        pl.semaphore_signal(barrier, inc=1, device_id=(lax.rem(row + d, ROWS), col), device_id_type=MESH)

    def greet_col(d):
        pl.semaphore_signal(barrier, inc=1, device_id=(row, lax.rem(col + d, COLS)), device_id_type=MESH)

    loop(1, ROWS, greet_row)
    loop(1, COLS, greet_col)

    for load in loads[:5]:
        load.wait()
    own = jnp.dot(src_ref[...], weight_ref[...], preferred_element_type=jnp.float32).astype(jnp.bfloat16)
    u_ref[row] = own[:, :BLK]
    v_ref[row] = own[:, BLK:]
    head_of = lax.broadcasted_iota(jnp.int32, (8, WIDTH), 1) // HD
    pick = head_of == lax.broadcasted_iota(jnp.int32, (8, WIDTH), 0)
    parts = in_three(jnp.where(pick, flat_scores(source_ref), 0.0))
    logits = [lax.dot_general(part, own, by_columns, preferred_element_type=jnp.float32) for part in parts]
    src_rows[row] = in_half(logits[0] + logits[1] + logits[2], row)
    product = jnp.dot(tgt_ref[...], weight_ref[...], preferred_element_type=jnp.float32) * flat_scores(target_ref)
    ones = pick.astype(jnp.bfloat16)
    logits = [lax.dot_general(ones, part, by_columns, preferred_element_type=jnp.float32) for part in in_three(product)]
    dst_rows[col] = in_half(logits[0] + logits[1] + logits[2], col)
    pl.semaphore_wait(barrier, ROWS + COLS - 2)

    def source_logits(d):
        return pltpu.make_async_remote_copy(
            src_ref=src_rows.at[row], dst_ref=src_rows.at[row], send_sem=send_a.at[d], recv_sem=recv_a.at[d],
            device_id=(lax.rem(row + d, ROWS), col), device_id_type=MESH,
        )

    def target_logits(d):
        return pltpu.make_async_remote_copy(
            src_ref=dst_rows.at[col], dst_ref=dst_rows.at[col], send_sem=send_b.at[d], recv_sem=recv_b.at[d],
            device_id=(row, lax.rem(col + d, COLS)), device_id_type=MESH,
        )

    def along_x(d):
        return pltpu.make_async_remote_copy(
            src_ref=u_ref.at[row], dst_ref=u_ref.at[row], send_sem=send_x.at[d], recv_sem=recv_x.at[d],
            device_id=(y * XS + lax.rem(x + d, XS), col), device_id_type=MESH,
        )

    def along_y(d):
        return pltpu.make_async_remote_copy(
            src_ref=v_ref.at[row], dst_ref=v_ref.at[row], send_sem=send_y.at[d], recv_sem=recv_y.at[d],
            device_id=(lax.rem(y + d, YS) * XS + x, col), device_id_type=MESH,
        )

    def up(k):
        first = lax.rem(y - (k - 1) + YS, YS) * XS
        part = pl.ds(first, XS if k < YS // 2 else XS // 2)
        return pltpu.make_async_remote_copy(
            src_ref=u_ref.at[part], dst_ref=u_ref.at[part], send_sem=send_up.at[k], recv_sem=recv_up.at[k],
            device_id=(lax.rem(y + 1, YS) * XS + x, col), device_id_type=MESH,
        )

    def down(k):
        first = lax.rem(y + (k - 1), YS) * XS
        part = pl.ds(first, XS) if k < YS // 2 else pl.ds(first + XS // 2, XS // 2)
        return pltpu.make_async_remote_copy(
            src_ref=u_ref.at[part], dst_ref=u_ref.at[part], send_sem=send_down.at[k], recv_sem=recv_down.at[k],
            device_id=(lax.rem(y + YS - 1, YS) * XS + x, col), device_id_type=MESH,
        )

    def onward(d, e):
        block = lax.rem(y - d + YS, YS) * XS + x
        return pltpu.make_async_remote_copy(
            src_ref=v_ref.at[block], dst_ref=v_ref.at[block], send_sem=send_f.at[d, e], recv_sem=recv_f.at[d, e],
            device_id=(y * XS + lax.rem(x + e, XS), col), device_id_type=MESH,
        )

    def hand_on(d):
        along_y(d).wait_recv()
        for e in range(1, XS):
            onward(d, e).start()

    def ring(k):
        if k > 1:
            up(k - 1).wait_recv()
            down(k - 1).wait_recv()
        up(k).start()
        down(k).start()

    loop(1, ROWS, lambda d: source_logits(d).start())
    for d in range(1, XS):
        along_x(d).start()
        onward(0, d).start()
    for d in (1, 7, 2, 6, 3, 5, 4):
        along_y(d).start()
    loop(1, COLS, lambda d: target_logits(d).start())

    for load in loads[5:]:
        load.wait()
    live = live_ref[0, 0]
    for d in range(1, XS):
        along_x(d).wait_recv()
    ring(1)
    loop(1, ROWS, lambda d: source_logits(d).wait_recv())
    everyone = jnp.concatenate([src_rows[2 * s] + src_rows[2 * s + 1] for s in range(SB)], axis=0).T
    for s in range(SB):
        for h in range(HEADS):
            spread[h, s] = jnp.broadcast_to(everyone[:, 8 * s + h : 8 * s + h + 1], (BLK, BLK))
    hand_on(1)
    hand_on(7)
    ring(2)

    bit = jnp.left_shift(1, lax.broadcasted_iota(jnp.int32, (8, BLK), 0))

    def edges(slot, w, bit):
        words = bits_ref[slot, pl.ds(w, 1), :]
        return (jnp.broadcast_to(words, (8, BLK)) & bit) != 0

    def slot_max(slot):
        s = slots_ref[0, slot] & (SB - 1)
        used = bit & (jnp.clip(live - slot, 0, 1) * 255)
        top = [jnp.full((8, BLK), no_edge, jnp.float32)] * HEADS
        for w in range(BLK // 8):
            mask = edges(slot, w, used)
            for h in range(HEADS):
                top[h] = jnp.maximum(top[h], jnp.where(mask, spread[h, s, 8 * w : 8 * w + 8, :], no_edge))
        for h in range(HEADS):
            tops[slot, h] = top[h]

    loop(0, SLOTS // 2, slot_max)
    for d in (2, 6, 3, 5, 4):
        hand_on(d)
    ring(3)
    loop(SLOTS // 2, SLOTS, slot_max)

    for h in range(HEADS):
        def widen(slot, found):
            d_here = jnp.full((8, BLK), jnp.right_shift(slots_ref[0, slot], 4), jnp.int32)
            top = tops[slot, h]
            return tuple(
                jnp.maximum(old, jnp.where(d_here == d, top, no_edge)) for d, old in enumerate(found)
            )

        found = lax.fori_loop(0, SLOTS, widen, (jnp.full((8, BLK), no_edge, jnp.float32),) * DB)
        for d in range(DB):
            best[d, h] = found[d]
    loop(1, COLS, lambda d: target_logits(d).wait_recv())
    for d in range(DB):
        dst[d] = dst_rows[2 * d] + dst_rows[2 * d + 1]
        values = []
        for h in range(HEADS):
            top = jnp.max(best[d, h], axis=0, keepdims=True)
            values.append(jnp.where(top > -1e38, leaky(top + dst[d, h : h + 1, :]), very_low))
        maxima_ref[d] = jnp.concatenate(values * 2, axis=0)
    ring(4)

    def slot_weights(slot):
        place = slots_ref[0, slot]
        d, s = jnp.right_shift(place, 4), place & (SB - 1)
        used = bit & (jnp.clip(live - slot, 0, 1) * 255)
        sums = [jnp.zeros((8, BLK), jnp.float32)] * HEADS
        b = [jnp.broadcast_to(dst[d, h : h + 1, :], (8, BLK)) for h in range(HEADS)]
        m = [jnp.broadcast_to(maxima_ref[d, h : h + 1, :], (8, BLK)) for h in range(HEADS)]
        for w in range(0, BLK // 8, 2):
            masks = [edges(slot, w, used), edges(slot, w + 1, used)]
            for h in range(HEADS):
                pair = []
                for half in range(2):
                    from_src = spread[h, s, 8 * (w + half) : 8 * (w + half) + 8, :]
                    score = leaky(from_src + b[h]) - m[h]
                    numer = jnp.where(masks[half], jnp.exp(score), 0.0)
                    sums[h] = sums[h] + numer
                    pair.append(numer)
                weights_ref[slot, h, 8 * w : 8 * w + 16, :] = jnp.concatenate(pair, axis=0).astype(jnp.bfloat16)
        for h in range(HEADS):
            sums_ref[slot, h] = sums[h]

    loop(0, SLOTS, slot_weights)

    loop(1, ROWS, lambda d: source_logits(d).wait_send())
    loop(1, COLS, lambda d: target_logits(d).wait_send())
    for d in range(1, XS):
        along_x(d).wait_send()
    for k in range(1, YS // 2 + 1):
        up(k).wait_send()
        down(k).wait_send()
    up(YS // 2).wait_recv()
    down(YS // 2).wait_recv()
    for d in range(YS):
        if d:
            along_y(d).wait_send()
        for e in range(1, XS):
            onward(d, e).wait()


def scores(source, target, weight, score_source, score_target, slots, live, bits):
    vmem = pl.BlockSpec(memory_space=pltpu.VMEM)
    anywhere = pl.BlockSpec(memory_space=pl.ANY)
    dma = pltpu.SemaphoreType.DMA
    return pl.pallas_call(
        scores_kernel,
        out_shape=(
            jax.ShapeDtypeStruct((ROWS, OWN, BLK), jnp.bfloat16),
            jax.ShapeDtypeStruct((ROWS, OWN, BLK), jnp.bfloat16),
            jax.ShapeDtypeStruct((SLOTS, HEADS, BLK, BLK), jnp.bfloat16),
            jax.ShapeDtypeStruct((SLOTS, HEADS, 8, BLK), jnp.float32),
            jax.ShapeDtypeStruct((DB, 8, BLK), jnp.float32),
        ),
        in_specs=[anywhere] * 8,
        out_specs=(vmem,) * 5,
        scratch_shapes=[
            pltpu.VMEM((OWN, WIDTH), jnp.bfloat16),
            pltpu.VMEM((OWN, WIDTH), jnp.bfloat16),
            pltpu.VMEM((WIDTH, WIDTH), jnp.bfloat16),
            pltpu.VMEM((HEADS, HD), jnp.float32),
            pltpu.VMEM((HEADS, HD), jnp.float32),
            pltpu.SMEM((1, SLOTS), jnp.int32),
            pltpu.SMEM((1, 1), jnp.int32),
            pltpu.VMEM((SLOTS, BLK // 8, BLK), jnp.int32),
            pltpu.VMEM((ROWS, 8, BLK), jnp.float32),
            pltpu.VMEM((COLS, 8, BLK), jnp.float32),
            pltpu.VMEM((HEADS, SB, BLK, BLK), jnp.float32),
            pltpu.VMEM((DB, 8, BLK), jnp.float32),
            pltpu.VMEM((SLOTS, HEADS, 8, BLK), jnp.float32),
            pltpu.VMEM((DB, HEADS, 8, BLK), jnp.float32),
            dma((8,)),
            dma((ROWS,)), dma((ROWS,)),
            dma((COLS,)), dma((COLS,)),
            dma((XS,)), dma((XS,)),
            dma((YS,)), dma((YS,)),
            dma((YS,)), dma((YS,)),
            dma((YS,)), dma((YS,)),
            dma((YS, XS)), dma((YS, XS)),
        ],
        compiler_params=pltpu.CompilerParams(collective_id=0, has_side_effects=True, vmem_limit_bytes=32 << 20),
        name="scores",
    )(source, target, weight, score_source, score_target, slots, live, bits)


def sums_kernel(slots_ref, u_ref, v_ref, weights_ref, parts_ref, maxima_ref, accum_ref, stats_ref, turned, accum, total):
    eye = (
        lax.broadcasted_iota(jnp.int32, (BLK, BLK), 0) == lax.broadcasted_iota(jnp.int32, (BLK, BLK), 1)
    ).astype(jnp.bfloat16)
    for s in range(SB):
        for i, ref in enumerate((u_ref, v_ref)):
            block = ref[s * BLK : (s + 1) * BLK, :]
            flipped = lax.dot_general(eye, block, by_columns, preferred_element_type=jnp.float32)
            turned[s, i * BLK : (i + 1) * BLK, :] = flipped.astype(jnp.bfloat16)
    total[...] = jnp.zeros(total.shape, jnp.float32)
    accum[...] = jnp.zeros(accum.shape, jnp.float32)

    @pl.loop(0, SLOTS, unroll=UNROLL)
    def _(slot):
        place = slots_ref[0, slot]
        d, s = place // SB, lax.rem(place, SB)
        for h in range(HEADS):
            part = jnp.dot(turned[s, h * HD : (h + 1) * HD, :], weights_ref[slot, h], preferred_element_type=jnp.float32)
            accum[d, h * HD : (h + 1) * HD, :] += part
            total[d, h] += parts_ref[slot, h]

    for d in range(DB):
        accum_ref[d] = accum[d].astype(jnp.bfloat16)
        rows = [maxima_ref[d, :HEADS, :]] + [jnp.sum(total[d, h], axis=0, keepdims=True) for h in range(HEADS)]
        stats_ref[d] = jnp.concatenate(rows, axis=0)


UNROLL = 4


def sums(slots, u, v, weights, parts, maxima):
    vmem = pl.BlockSpec(memory_space=pltpu.VMEM)
    smem = pl.BlockSpec(memory_space=pltpu.SMEM)
    return pl.pallas_call(
        sums_kernel,
        out_shape=(
            jax.ShapeDtypeStruct((DB, WIDTH, BLK), jnp.bfloat16),
            jax.ShapeDtypeStruct((DB, 8, BLK), jnp.float32),
        ),
        in_specs=[smem] + [vmem] * 5,
        out_specs=(vmem, vmem),
        scratch_shapes=[
            pltpu.VMEM((SB, WIDTH, BLK), jnp.bfloat16),
            pltpu.VMEM((DB, WIDTH, BLK), jnp.float32),
            pltpu.VMEM((DB, HEADS, 8, BLK), jnp.float32),
        ],
        compiler_params=pltpu.CompilerParams(vmem_limit_bytes=24 << 20),
        name="sums",
    )(slots, u, v, weights, parts, maxima)


def combine_kernel(
    accum_ref, stats_ref, bias_ref, out_ref, twin_accum, twin_stats, got, got_stats, half_ref, twin_half,
    send_p, recv_p, send_q, recv_q, send_a, recv_a, send_b, recv_b, send_o, recv_o, joint, joint_stats,
):
    row, col = lax.axis_index("row"), lax.axis_index("col")
    z, core = col // 2, lax.rem(col, 2)
    twin = (row, col + 1 - 2 * core)
    barrier = pltpu.get_barrier_semaphore()
    pl.semaphore_signal(barrier, inc=1, device_id=twin, device_id_type=MESH)

    def peer(d):
        return (row, lax.rem(z + d, ZS) * 2 + core)

    loop(1, ZS, lambda d: pl.semaphore_signal(barrier, inc=1, device_id=peer(d), device_id_type=MESH))
    pl.semaphore_wait(barrier, ZS)

    theirs = pl.ds(pl.multiple_of((1 - core) * BLK, BLK), BLK)
    mine = pl.ds(pl.multiple_of(core * BLK, BLK), BLK)

    def stats_copy():
        return pltpu.make_async_remote_copy(
            src_ref=stats_ref, dst_ref=twin_stats, send_sem=send_q, recv_sem=recv_q, device_id=twin, device_id_type=MESH,
        )

    def pair_copy(d):
        return pltpu.make_async_remote_copy(
            src_ref=accum_ref.at[d, theirs], dst_ref=twin_accum.at[d], send_sem=send_p.at[d], recv_sem=recv_p.at[d],
            device_id=twin, device_id_type=MESH,
        )

    def joint_copy(d):
        there = lax.rem(z + d, ZS)
        return pltpu.make_async_remote_copy(
            src_ref=joint.at[there], dst_ref=got.at[z], send_sem=send_a.at[d], recv_sem=recv_a.at[d],
            device_id=peer(d), device_id_type=MESH,
        )

    def joint_stats_copy(d):
        there = lax.rem(z + d, ZS)
        return pltpu.make_async_remote_copy(
            src_ref=joint_stats.at[there], dst_ref=got_stats.at[z], send_sem=send_b.at[d], recv_sem=recv_b.at[d],
            device_id=peer(d), device_id_type=MESH,
        )

    order = (4, 3, 5, 2, 6, 1, 7, 0)
    stats_copy().start()
    for d in order:
        pair_copy(lax.rem(z + d, ZS)).start()
    stats_copy().wait_recv()

    def own_heads(tile):
        return jnp.where(core == 0, tile[0:2], tile[2:4]), jnp.where(core == 0, tile[4:6], tile[6:8])

    for d in order:
        there = lax.rem(z + d, ZS)
        m0, s0 = own_heads(stats_ref[there])
        m1, s1 = own_heads(twin_stats[there])
        m = jnp.maximum(m0, m1)
        f0, f1 = jnp.exp(m0 - m), jnp.exp(m1 - m)
        tile = jnp.concatenate([m, s0 * f0 + s1 * f1, m, m], axis=0)
        pair_copy(there).wait_recv()
        mixed = []
        for h in range(2):
            rows = pl.ds(pl.multiple_of(core * BLK + h * HD, HD), HD)
            mine_part = accum_ref[there, rows, :].astype(jnp.float32)
            twin_part = twin_accum[there, h * HD : (h + 1) * HD, :].astype(jnp.float32)
            mixed.append(mine_part * f0[h : h + 1] + twin_part * f1[h : h + 1])
        mixed = jnp.concatenate(mixed, axis=0).astype(jnp.bfloat16)
        if d:
            joint_stats[there] = tile
            joint[there] = mixed
            joint_stats_copy(d).start()
            joint_copy(d).start()
        else:
            got_stats[z] = tile
            got[z] = mixed

    for d in range(1, ZS):
        joint_stats_copy(d).wait_recv()
    every = got_stats[...]
    local = every[:, 0:2, :]
    top = jnp.max(local, axis=0, keepdims=True)
    factor = jnp.exp(local - top)
    denoms = jnp.sum(factor * every[:, 2:4, :], axis=0, keepdims=True)
    factor = factor / jnp.maximum(denoms, 1.0)
    for d in range(1, ZS):
        joint_copy(d).wait_recv()
    parts = []
    for h in range(2):
        part = jnp.zeros((HD, BLK), jnp.float32)
        for c in range(ZS):
            part = part + factor[c, h : h + 1, :] * got[c, h * HD : (h + 1) * HD, :].astype(jnp.float32)
        parts.append(part)
    turned = jnp.concatenate(parts, axis=0).T
    bias = jnp.where(core == 0, bias_ref[:, :BLK], bias_ref[:, BLK:])
    blended = turned + bias
    result = jnp.where(blended > 0, blended, jnp.exp(jnp.minimum(blended, 0.0)) - 1.0).astype(jnp.bfloat16)
    half_ref[...] = jnp.where(core == 0, result[OWN:], result[:OWN])
    swap = pltpu.make_async_remote_copy(
        src_ref=half_ref, dst_ref=twin_half, send_sem=send_o, recv_sem=recv_o, device_id=twin, device_id_type=MESH,
    )
    swap.start()
    out_ref[:, mine] = jnp.where(core == 0, result[:OWN], result[OWN:])
    for d in range(1, ZS):
        joint_stats_copy(d).wait_send()
        joint_copy(d).wait_send()
    stats_copy().wait_send()
    loop(0, ZS, lambda d: pair_copy(d).wait_send())
    swap.wait()
    out_ref[:, theirs] = twin_half[...]


def combine(accum, stats, bias):
    vmem = pl.BlockSpec(memory_space=pltpu.VMEM)
    dma = pltpu.SemaphoreType.DMA
    return pl.pallas_call(
        combine_kernel,
        out_shape=jax.ShapeDtypeStruct((OWN, WIDTH), jnp.bfloat16),
        in_specs=[vmem] * 3,
        out_specs=vmem,
        scratch_shapes=[
            pltpu.VMEM((ZS, BLK, BLK), jnp.bfloat16),
            pltpu.VMEM((ZS, 8, BLK), jnp.float32),
            pltpu.VMEM((ZS, BLK, BLK), jnp.bfloat16),
            pltpu.VMEM((ZS, 8, BLK), jnp.float32),
            pltpu.VMEM((OWN, BLK), jnp.bfloat16),
            pltpu.VMEM((OWN, BLK), jnp.bfloat16),
            dma((ZS,)), dma((ZS,)),
            dma, dma,
            dma((ZS,)), dma((ZS,)),
            dma((ZS,)), dma((ZS,)),
            dma, dma,
            pltpu.VMEM((ZS, BLK, BLK), jnp.bfloat16),
            pltpu.VMEM((ZS, 8, BLK), jnp.float32),
        ],
        compiler_params=pltpu.CompilerParams(collective_id=1, has_side_effects=True, vmem_limit_bytes=16 << 20),
        name="combine",
    )(accum, stats, bias)


def body(
    source_features, target_features, weight, score_source, score_target, out_bias,
    block_list, block_count, edge_bits,
):
    slots = block_list[0]
    u, v, weights, parts, maxima = scores(
        source_features[0], target_features, weight, score_source, score_target, slots, block_count, edge_bits[0, 0]
    )
    flat = (SB * BLK, BLK)
    accum, stats = sums(slots, u.reshape(flat), v.reshape(flat), weights, parts, maxima)
    return combine(accum, stats, out_bias.reshape(1, WIDTH))


def solution(mesh):
    placed = (
        P("col", "row", None),
        P(("row", "col"), None),
        P(),
        P(),
        P(),
        P(),
        P("row", "col", None),
        P("row", "col"),
        P("row", "col", None, None, None),
    )
    return jax.shard_map(
        body, mesh=mesh, in_specs=placed, out_specs=P(("row", "col"), None), check_vma=False
    )
```

```python
import jax
import jax.numpy as jnp
from jax import lax
from jax.experimental import pallas as pl
from jax.experimental.pallas import tpu as pltpu
from jax.sharding import PartitionSpec as P

BLK = 128
SB = 16
DB = 8
SLOTS = 48
HEADS = 4
HD = 64
WIDTH = 256
ROWS = 32
COLS = 16
XS = 4
YS = 8
ZS = 8
OWN = 64

very_low = -1e30
no_edge = -3e38
slope = 0.2
MESH = pl.DeviceIdType.MESH
by_columns = (((1,), (1,)), ((), ()))


def in_three(x):
    high = x.astype(jnp.bfloat16)
    rest = x - high.astype(jnp.float32)
    middle = rest.astype(jnp.bfloat16)
    low = (rest - middle.astype(jnp.float32)).astype(jnp.bfloat16)
    return low, middle, high


def leaky(x):
    return jnp.maximum(x, slope * x)


def loop(first, last, step):
    def one(i, _):
        step(i)
        return 0

    lax.fori_loop(first, last, one, 0)


def in_half(rows, position):
    twice = jnp.concatenate([rows, rows], axis=1)
    half = lax.broadcasted_iota(jnp.int32, (HEADS, BLK), 1) // OWN
    return jnp.where(half == lax.rem(position, 2), twice[:HEADS], 0.0)


def flat_scores(ref):
    return jnp.concatenate([ref[h : h + 1, :] for h in range(HEADS)], axis=1)


def layer_kernel(
    src_hbm, tgt_hbm, weight_hbm, source_hbm, target_hbm, bias_hbm, slots_hbm, live_hbm, bits_hbm,
    out_ref,
    src_ref, tgt_ref, weight_ref, source_ref, target_ref, bias_ref, slots_ref, live_ref, bits_ref,
    feats, src_rows, dst_half, dst, place_rows, places, everyone, spread, tops, maxima, turned,
    even, odd, slot_sums, products, accum, sent, stats, twin_sent, twin_stats,
    joint, joint_stats, got, got_stats, half_ref, twin_half,
    local, send_ay, recv_ay, send_ax, recv_ax, send_b, recv_b, send_y, recv_y, send_x, recv_x,
    send_p, recv_p, send_j, recv_j, send_k, recv_k, send_one, recv_one,
):
    row, col = lax.axis_index("row"), lax.axis_index("col")
    x, y = lax.rem(row, XS), row // XS
    z, core = col // 2, lax.rem(col, 2)
    twin = (row, col + 1 - 2 * core)
    pairs = (
        (weight_hbm, weight_ref), (src_hbm, src_ref), (source_hbm, source_ref), (tgt_hbm, tgt_ref),
        (target_hbm, target_ref), (slots_hbm, slots_ref), (live_hbm, live_ref), (bits_hbm, bits_ref),
        (bias_hbm, bias_ref),
    )
    loads = [pltpu.make_async_copy(a, b, local.at[i]) for i, (a, b) in enumerate(pairs)]
    for load in loads:
        load.start()

    def at_x(d):
        return (y * XS + lax.rem(x + d, XS), col)

    def at_y(d):
        return (lax.rem(y + d, YS) * XS + x, col)

    def at_z(d):
        return (row, lax.rem(z + d, ZS) * 2 + core)

    barrier = pltpu.get_barrier_semaphore()
    for d in range(1, YS):
        pl.semaphore_signal(barrier, inc=1, device_id=at_y(d), device_id_type=MESH)
    for d in range(1, XS):
        pl.semaphore_signal(barrier, inc=1, device_id=at_x(d), device_id_type=MESH)
    for d in range(1, ZS):
        pl.semaphore_signal(barrier, inc=1, device_id=at_z(d), device_id_type=MESH)
    pl.semaphore_signal(barrier, inc=1, device_id=twin, device_id_type=MESH)

    def send(source, target, semaphores, device):
        return pltpu.make_async_remote_copy(
            src_ref=source, dst_ref=target, send_sem=semaphores[0], recv_sem=semaphores[1],
            device_id=device, device_id_type=MESH,
        )

    def logits_y(d):
        return send(src_rows.at[x, y], src_rows.at[x, y], (send_ay.at[d], recv_ay.at[d]), at_y(d))

    def logits_x(d):
        return send(src_rows.at[x], src_rows.at[x], (send_ax.at[d], recv_ax.at[d]), at_x(d))

    def feats_y(d):
        return send(feats.at[row], feats.at[row], (send_y.at[d], recv_y.at[d]), at_y(d))

    def feats_x(d, e):
        block = lax.rem(y - d + YS, YS) * XS + x
        return send(feats.at[block], feats.at[block], (send_x.at[d, e], recv_x.at[d, e]), at_x(e))

    def target_pair():
        return send(dst_half.at[0], dst_half.at[1], (send_one.at[0], recv_one.at[0]), twin)

    def target_z(d):
        return send(dst.at[z], dst.at[z], (send_b.at[d], recv_b.at[d]), at_z(d))

    def stats_pair():
        return send(stats, twin_stats, (send_one.at[1], recv_one.at[1]), twin)

    def sums_pair(d):
        theirs = pl.ds(pl.multiple_of((1 - core) * BLK, BLK), BLK)
        return send(sent.at[d, theirs], twin_sent.at[d], (send_p.at[d], recv_p.at[d]), twin)

    def sums_z(d):
        return send(joint.at[lax.rem(z + d, ZS)], got.at[z], (send_j.at[d], recv_j.at[d]), at_z(d))

    def stats_z(d):
        return send(joint_stats.at[lax.rem(z + d, ZS)], got_stats.at[z], (send_k.at[d], recv_k.at[d]), at_z(d))

    def result_pair():
        return send(half_ref, twin_half, (send_one.at[2], recv_one.at[2]), twin)

    for load in loads[:3]:
        load.wait()
    own = jnp.dot(src_ref[...], weight_ref[...], preferred_element_type=jnp.float32).astype(jnp.bfloat16)
    feats[row] = own
    head_of = lax.broadcasted_iota(jnp.int32, (8, WIDTH), 1) // HD
    pick = head_of == lax.broadcasted_iota(jnp.int32, (8, WIDTH), 0)
    parts = jnp.concatenate(in_three(jnp.where(pick, flat_scores(source_ref), 0.0)), axis=0)
    logits = lax.dot_general(parts, own, by_columns, preferred_element_type=jnp.float32)
    src_rows[x, y] = in_half(logits[0:8] + logits[8:16] + logits[16:24], row)
    pl.semaphore_wait(barrier, XS + YS + ZS - 2)

    far_first = (4, 3, 5, 2, 6, 1, 7)
    near_first = (1, 7, 2, 6, 3, 5, 4)
    for d in far_first:
        logits_y(d).start()
    for d in far_first:
        feats_y(d).start()
    for e in range(1, XS):
        feats_x(0, e).start()

    for load in loads[3:5]:
        load.wait()
    product = jnp.dot(tgt_ref[...], weight_ref[...], preferred_element_type=jnp.float32) * flat_scores(target_ref)
    ones = pick.astype(jnp.bfloat16)
    logits = [lax.dot_general(ones, part, by_columns, preferred_element_type=jnp.float32) for part in in_three(product)]
    dst_half[0] = in_half(logits[0] + logits[1] + logits[2], col)
    target_pair().start()

    for load in loads[5:]:
        load.wait()
    live = live_ref[0, 0]
    lane = lax.broadcasted_iota(jnp.int32, (1, BLK), 1)

    def put(slot, table):
        name = slots_ref[0, slot] + BLK * jnp.clip(slot + 1 - live, 0, 1)
        return jnp.where(lane == jnp.full((1, BLK), name, jnp.int32), slot, table)

    place_rows[...] = lax.fori_loop(0, SLOTS, put, jnp.full((1, BLK), SLOTS, jnp.int32), unroll=8)
    table = pltpu.make_async_copy(place_rows, places, local.at[9])
    table.start()
    everyone[...] = jnp.zeros(everyone.shape, jnp.float32)
    tops[SLOTS] = jnp.full((HEADS, 8, BLK), no_edge, jnp.float32)
    slot_sums[SLOTS] = jnp.zeros((HEADS, 8, BLK), jnp.float32)
    products[SLOTS] = jnp.zeros((WIDTH, BLK), jnp.float32)
    odd[...] = jnp.zeros(odd.shape, jnp.bfloat16)
    target_pair().wait_recv()
    dst[z] = dst_half[0] + dst_half[1]
    for d in range(1, ZS):
        target_z(d).start()

    for d in near_first:
        logits_y(d).wait_recv()
    for e in range(1, XS):
        logits_x(e).start()
    for d in near_first:
        feats_y(d).wait_recv()
        for e in range(1, XS):
            feats_x(d, e).start()
    for e in range(1, XS):
        logits_x(e).wait_recv()
    for s in range(SB):
        here, pair = s // 2, (s % 2) * 2
        everyone[8 * s : 8 * s + HEADS, :] = src_rows[pair, here] + src_rows[pair + 1, here]
    columns = everyone[...].T
    for s in range(SB):
        for h in range(HEADS):
            spread[h, s] = jnp.broadcast_to(columns[:, 8 * s + h : 8 * s + h + 1], (BLK, BLK))

    bit = jnp.left_shift(1, lax.broadcasted_iota(jnp.int32, (8, BLK), 0))

    def edges(slot, w):
        words = bits_ref[slot, pl.ds(w, 1), :]
        return (jnp.broadcast_to(words, (8, BLK)) & bit) != 0

    def slot_max(slot):
        s = slots_ref[0, slot] & (SB - 1)
        top = [jnp.full((8, BLK), no_edge, jnp.float32)] * HEADS
        for w in range(BLK // 8):
            mask = edges(slot, w)
            for h in range(HEADS):
                top[h] = jnp.maximum(top[h], jnp.where(mask, spread[h, s, 8 * w : 8 * w + 8, :], no_edge))
        for h in range(HEADS):
            tops[slot, h] = top[h]

    loop(0, SLOTS, slot_max)
    table.wait()
    for d in range(1, ZS):
        target_z(d).wait_recv()

    def block_max(d):
        best = [tops[places[0, d * SB], h] for h in range(HEADS)]
        for k in range(1, SB):
            slot = places[0, d * SB + k]
            best = [jnp.maximum(best[h], tops[slot, h]) for h in range(HEADS)]
        for h in range(HEADS):
            top = jnp.max(best[h], axis=0, keepdims=True)
            maxima[d, h : h + 1, :] = jnp.where(top > -1e38, leaky(top + dst[d, h : h + 1, :]), very_low)

    loop(0, DB, block_max)

    for d in range(YS):
        for e in range(1, XS):
            feats_x(d, e).wait_recv()
    eye = (
        lax.broadcasted_iota(jnp.int32, (WIDTH, WIDTH), 0) == lax.broadcasted_iota(jnp.int32, (WIDTH, WIDTH), 1)
    ).astype(jnp.bfloat16)

    def turn(s):
        block = jnp.concatenate([feats[2 * s], feats[2 * s + 1]], axis=0)
        turned[s] = lax.dot_general(eye, block, by_columns, preferred_element_type=jnp.float32).astype(jnp.bfloat16)

    loop(0, SB, turn)

    def slot_weights(slot, weights):
        place = slots_ref[0, slot]
        d, s = jnp.right_shift(place, 4), place & (SB - 1)
        sums = [jnp.zeros((8, BLK), jnp.float32)] * HEADS
        b = [jnp.broadcast_to(dst[d, h : h + 1, :], (8, BLK)) for h in range(HEADS)]
        m = [jnp.broadcast_to(maxima[d, h : h + 1, :], (8, BLK)) for h in range(HEADS)]
        for w in range(0, BLK // 8, 2):
            masks = [edges(slot, w), edges(slot, w + 1)]
            for h in range(HEADS):
                pair = []
                for half in range(2):
                    from_src = spread[h, s, 8 * (w + half) : 8 * (w + half) + 8, :]
                    score = leaky(from_src + b[h]) - m[h]
                    numer = jnp.where(masks[half], jnp.exp(score), 0.0)
                    sums[h] = sums[h] + numer
                    pair.append(numer)
                weights[h, 8 * w : 8 * w + 16, :] = jnp.concatenate(pair, axis=0).astype(jnp.bfloat16)
        for h in range(HEADS):
            slot_sums[slot, h] = sums[h]

    def slot_product(slot, weights):
        s = slots_ref[0, slot] & (SB - 1)
        for h in range(HEADS):
            rows = slice(h * HD, (h + 1) * HD)
            products[slot, rows, :] = jnp.dot(turned[s, rows, :], weights[h], preferred_element_type=jnp.float32)

    def two_slots(i):
        slot_product(jnp.maximum(2 * i - 1, 0), odd)
        slot_weights(2 * i, even)
        slot_product(2 * i, even)
        slot_weights(2 * i + 1, odd)

    loop(0, SLOTS // 2, two_slots)
    slot_product(SLOTS - 1, odd)

    def block_stats(d):
        total = [slot_sums[places[0, d * SB], h] for h in range(HEADS)]
        for k in range(1, SB):
            slot = places[0, d * SB + k]
            total = [total[h] + slot_sums[slot, h] for h in range(HEADS)]
        rows = [maxima[d]] + [jnp.sum(total[h], axis=0, keepdims=True) for h in range(HEADS)]
        stats[d] = jnp.concatenate(rows, axis=0)

    loop(0, DB, block_stats)
    stats_pair().start()
    order = (4, 3, 5, 2, 6, 1, 7, 0)
    for o in order:
        d = lax.rem(z + o, ZS)

        def add(k, total):
            for i in range(4):
                total = total + products[places[0, d * SB + 4 * k + i]]
            return total

        total = lax.fori_loop(0, SB // 4, add, jnp.zeros((WIDTH, BLK), jnp.float32))
        accum[d] = total
        sent[d] = total.astype(jnp.bfloat16)
        sums_pair(d).start()
    stats_pair().wait_recv()

    def own_heads(tile):
        return jnp.where(core == 0, tile[0:2], tile[2:4]), jnp.where(core == 0, tile[4:6], tile[6:8])

    for o in order:
        d = lax.rem(z + o, ZS)
        m0, s0 = own_heads(stats[d])
        m1, s1 = own_heads(twin_stats[d])
        m = jnp.maximum(m0, m1)
        f0, f1 = jnp.exp(m0 - m), jnp.exp(m1 - m)
        tile = jnp.concatenate([m, s0 * f0 + s1 * f1, m, m], axis=0)
        sums_pair(d).wait_recv()
        mixed = []
        for h in range(2):
            rows = pl.ds(pl.multiple_of(core * BLK + h * HD, HD), HD)
            twin_part = twin_sent[d, h * HD : (h + 1) * HD, :].astype(jnp.float32)
            mixed.append(accum[d, rows, :] * f0[h : h + 1] + twin_part * f1[h : h + 1])
        mixed = jnp.concatenate(mixed, axis=0).astype(jnp.bfloat16)
        if o:
            joint_stats[d] = tile
            joint[d] = mixed
            stats_z(o).start()
            sums_z(o).start()
        else:
            got_stats[z] = tile
            got[z] = mixed

    for d in range(1, ZS):
        stats_z(d).wait_recv()
    every = got_stats[...]
    near = every[:, 0:2, :]
    factor = jnp.exp(near - jnp.max(near, axis=0, keepdims=True))
    denoms = jnp.sum(factor * every[:, 2:4, :], axis=0, keepdims=True)
    factor = factor / jnp.maximum(denoms, 1.0)
    for d in range(1, ZS):
        sums_z(d).wait_recv()
    parts = []
    for h in range(2):
        part = jnp.zeros((HD, BLK), jnp.float32)
        for c in range(ZS):
            part = part + factor[c, h : h + 1, :] * got[c, h * HD : (h + 1) * HD, :].astype(jnp.float32)
        parts.append(part)
    bias = jnp.where(core == 0, bias_ref[:, :BLK], bias_ref[:, BLK:])
    blended = jnp.concatenate(parts, axis=0).T + bias
    result = jnp.where(blended > 0, blended, jnp.exp(jnp.minimum(blended, 0.0)) - 1.0).astype(jnp.bfloat16)
    half_ref[...] = jnp.where(core == 0, result[OWN:], result[:OWN])
    result_pair().start()
    out_ref[:, pl.ds(pl.multiple_of(core * BLK, BLK), BLK)] = jnp.where(core == 0, result[:OWN], result[OWN:])

    for d in range(1, YS):
        logits_y(d).wait_send()
        feats_y(d).wait_send()
    for e in range(1, XS):
        logits_x(e).wait_send()
        for d in range(YS):
            feats_x(d, e).wait_send()
    target_pair().wait_send()
    stats_pair().wait_send()
    for d in range(1, ZS):
        target_z(d).wait_send()
        stats_z(d).wait_send()
        sums_z(d).wait_send()
    loop(0, ZS, lambda d: sums_pair(d).wait_send())
    result_pair().wait()
    out_ref[:, pl.ds(pl.multiple_of((1 - core) * BLK, BLK), BLK)] = twin_half[...]


def layer(source, target, weight, score_source, score_target, bias, slots, live, bits):
    dma = pltpu.SemaphoreType.DMA
    vmem = pltpu.VMEM
    f32, bf16 = jnp.float32, jnp.bfloat16
    return pl.pallas_call(
        layer_kernel,
        out_shape=jax.ShapeDtypeStruct((OWN, WIDTH), bf16),
        in_specs=[pl.BlockSpec(memory_space=pltpu.HBM)] * 9,
        out_specs=pl.BlockSpec(memory_space=pltpu.VMEM),
        scratch_shapes=[
            vmem((OWN, WIDTH), bf16),
            vmem((OWN, WIDTH), bf16),
            vmem((WIDTH, WIDTH), bf16),
            vmem((HEADS, HD), f32),
            vmem((HEADS, HD), f32),
            vmem((1, WIDTH), f32),
            pltpu.SMEM((1, SLOTS), jnp.int32),
            pltpu.SMEM((1, 1), jnp.int32),
            vmem((SLOTS, BLK // 8, BLK), jnp.int32),
            vmem((ROWS, OWN, WIDTH), bf16),
            vmem((XS, YS, HEADS, BLK), f32),
            vmem((2, HEADS, BLK), f32),
            vmem((DB, HEADS, BLK), f32),
            vmem((1, BLK), jnp.int32),
            pltpu.SMEM((1, BLK), jnp.int32),
            vmem((BLK, BLK), f32),
            vmem((HEADS, SB, BLK, BLK), f32),
            vmem((SLOTS + 1, HEADS, 8, BLK), f32),
            vmem((DB, HEADS, BLK), f32),
            vmem((SB, WIDTH, BLK), bf16),
            vmem((HEADS, BLK, BLK), bf16),
            vmem((HEADS, BLK, BLK), bf16),
            vmem((SLOTS + 1, HEADS, 8, BLK), f32),
            vmem((SLOTS + 1, WIDTH, BLK), f32),
            vmem((DB, WIDTH, BLK), f32),
            vmem((DB, WIDTH, BLK), bf16),
            vmem((DB, 8, BLK), f32),
            vmem((DB, BLK, BLK), bf16),
            vmem((DB, 8, BLK), f32),
            vmem((DB, BLK, BLK), bf16),
            vmem((DB, 8, BLK), f32),
            vmem((DB, BLK, BLK), bf16),
            vmem((DB, 8, BLK), f32),
            vmem((OWN, BLK), bf16),
            vmem((OWN, BLK), bf16),
            dma((10,)),
            dma((YS,)), dma((YS,)),
            dma((XS,)), dma((XS,)),
            dma((ZS,)), dma((ZS,)),
            dma((YS,)), dma((YS,)),
            dma((YS, XS)), dma((YS, XS)),
            dma((ZS,)), dma((ZS,)),
            dma((ZS,)), dma((ZS,)),
            dma((ZS,)), dma((ZS,)),
            dma((3,)), dma((3,)),
        ],
        compiler_params=pltpu.CompilerParams(collective_id=0, has_side_effects=True, vmem_limit_bytes=60 << 20),
        name="layer",
    )(source, target, weight, score_source, score_target, bias, slots, live, bits)


def body(
    source_features, target_features, weight, score_source, score_target, out_bias,
    block_list, block_count, edge_bits,
):
    return layer(
        source_features[0], target_features, weight, score_source, score_target, out_bias.reshape(1, WIDTH),
        block_list[0], block_count, edge_bits[0, 0],
    )


def solution(mesh):
    placed = (
        P("col", "row", None),
        P(("row", "col"), None),
        P(),
        P(),
        P(),
        P(),
        P("row", "col", None),
        P("row", "col"),
        P("row", "col", None, None, None),
    )
    return jax.shard_map(
        body, mesh=mesh, in_specs=placed, out_specs=P(("row", "col"), None), check_vma=False
    )
```

```python
import jax
import jax.numpy as jnp
from jax import lax
from jax.experimental import pallas as pl
from jax.experimental.pallas import tpu as pltpu
from jax.sharding import PartitionSpec as P

BLK = 128
SB = 16
DB = 8
SLOTS = 48
HEADS = 4
HD = 64
WIDTH = 256
ROWS = 32
COLS = 16
XS = 4
YS = 8
ZS = 8
OWN = 64

very_low = -1e30
no_edge = -3e38
slope = 0.2
log2e = 1.4426950408889634
MESH = pl.DeviceIdType.MESH
by_columns = (((1,), (1,)), ((), ()))


def in_three(x):
    high = x.astype(jnp.bfloat16)
    rest = x - high.astype(jnp.float32)
    middle = rest.astype(jnp.bfloat16)
    low = (rest - middle.astype(jnp.float32)).astype(jnp.bfloat16)
    return low, middle, high


def leaky(x):
    return jnp.maximum(x, slope * x)


def loop(first, last, step, unroll=1):
    def one(i, _):
        step(i)
        return 0

    lax.fori_loop(first, last, one, 0, unroll=unroll)


def in_half(rows, position):
    twice = jnp.concatenate([rows, rows], axis=1)
    half = lax.broadcasted_iota(jnp.int32, (HEADS, BLK), 1) // OWN
    return jnp.where(half == lax.rem(position, 2), twice[:HEADS], 0.0)


def flat_scores(ref):
    return jnp.concatenate([ref[h : h + 1, :] for h in range(HEADS)], axis=1)


def layer_kernel(
    src_hbm, tgt_hbm, weight_hbm, source_hbm, target_hbm, bias_hbm, slots_hbm, live_hbm, bits_hbm,
    out_ref,
    src_ref, tgt_ref, weight_ref, source_ref, target_ref, bias_ref, slots_ref, live_ref, bits_ref,
    feats, src_rows, dst_half, dst, place_rows, places, everyone, spread, tops, maxima, turned,
    weights, slot_sums, products, accum, sent, stats, twin_sent, twin_stats,
    joint, joint_stats, got, got_stats, half_ref, twin_half,
    local, send_ay, recv_ay, send_ax, recv_ax, send_b, recv_b, send_y, recv_y, send_x, recv_x,
    send_p, recv_p, send_j, recv_j, send_k, recv_k, send_one, recv_one,
):
    row, col = lax.axis_index("row"), lax.axis_index("col")
    x, y = lax.rem(row, XS), row // XS
    z, core = col // 2, lax.rem(col, 2)
    twin = (row, col + 1 - 2 * core)
    pairs = (
        (weight_hbm, weight_ref), (src_hbm, src_ref), (source_hbm, source_ref), (tgt_hbm, tgt_ref),
        (target_hbm, target_ref), (slots_hbm, slots_ref), (live_hbm, live_ref), (bits_hbm, bits_ref),
        (bias_hbm, bias_ref),
    )
    loads = [pltpu.make_async_copy(a, b, local.at[i]) for i, (a, b) in enumerate(pairs)]
    for load in loads:
        load.start()

    def at_x(d):
        return (y * XS + lax.rem(x + d, XS), col)

    def at_y(d):
        return (lax.rem(y + d, YS) * XS + x, col)

    def at_z(d):
        return (row, lax.rem(z + d, ZS) * 2 + core)

    barrier = pltpu.get_barrier_semaphore()
    for d in range(1, YS):
        pl.semaphore_signal(barrier, inc=1, device_id=at_y(d), device_id_type=MESH)
    for d in range(1, XS):
        pl.semaphore_signal(barrier, inc=1, device_id=at_x(d), device_id_type=MESH)
    for d in range(1, ZS):
        pl.semaphore_signal(barrier, inc=1, device_id=at_z(d), device_id_type=MESH)
    pl.semaphore_signal(barrier, inc=1, device_id=twin, device_id_type=MESH)

    def send(source, target, semaphores, device):
        return pltpu.make_async_remote_copy(
            src_ref=source, dst_ref=target, send_sem=semaphores[0], recv_sem=semaphores[1],
            device_id=device, device_id_type=MESH,
        )

    def logits_y(d):
        return send(src_rows.at[x, y], src_rows.at[x, y], (send_ay.at[d], recv_ay.at[d]), at_y(d))

    def logits_x(d):
        return send(src_rows.at[x], src_rows.at[x], (send_ax.at[d], recv_ax.at[d]), at_x(d))

    def feats_y(d):
        return send(feats.at[row], feats.at[row], (send_y.at[d], recv_y.at[d]), at_y(d))

    def feats_x(d, e):
        block = lax.rem(y - d + YS, YS) * XS + x
        return send(feats.at[block], feats.at[block], (send_x.at[d, e], recv_x.at[d, e]), at_x(e))

    def target_pair():
        return send(dst_half.at[0], dst_half.at[1], (send_one.at[0], recv_one.at[0]), twin)

    def target_z(d):
        return send(dst.at[z], dst.at[z], (send_b.at[d], recv_b.at[d]), at_z(d))

    def stats_pair():
        return send(stats, twin_stats, (send_one.at[1], recv_one.at[1]), twin)

    def sums_pair(d):
        theirs = pl.ds(pl.multiple_of((1 - core) * BLK, BLK), BLK)
        return send(sent.at[d, theirs], twin_sent.at[d], (send_p.at[d], recv_p.at[d]), twin)

    def sums_z(d):
        return send(joint.at[lax.rem(z + d, ZS)], got.at[z], (send_j.at[d], recv_j.at[d]), at_z(d))

    def stats_z(d):
        return send(joint_stats.at[lax.rem(z + d, ZS)], got_stats.at[z], (send_k.at[d], recv_k.at[d]), at_z(d))

    def result_pair():
        return send(half_ref, twin_half, (send_one.at[2], recv_one.at[2]), twin)

    for load in loads[:3]:
        load.wait()
    own = jnp.dot(src_ref[...], weight_ref[...], preferred_element_type=jnp.float32).astype(jnp.bfloat16)
    feats[row] = own
    head_of = lax.broadcasted_iota(jnp.int32, (8, WIDTH), 1) // HD
    pick = head_of == lax.broadcasted_iota(jnp.int32, (8, WIDTH), 0)
    parts = jnp.concatenate(in_three(jnp.where(pick, flat_scores(source_ref), 0.0)), axis=0)
    logits = lax.dot_general(parts, own, by_columns, preferred_element_type=jnp.float32)
    src_rows[x, y] = in_half((logits[0:8] + logits[8:16] + logits[16:24]) * log2e, row)
    pl.semaphore_wait(barrier, XS + YS + ZS - 2)

    far_first = (4, 3, 5, 2, 6, 1, 7)
    near_first = (1, 7, 2, 6, 3, 5, 4)
    for d in far_first:
        logits_y(d).start()
    for e in (2, 1, 3):
        feats_x(0, e).start()
    for d in near_first:
        feats_y(d).start()

    for load in loads[3:5]:
        load.wait()
    product = jnp.dot(tgt_ref[...], weight_ref[...], preferred_element_type=jnp.float32) * flat_scores(target_ref)
    ones = pick.astype(jnp.bfloat16)
    logits = [lax.dot_general(ones, part, by_columns, preferred_element_type=jnp.float32) for part in in_three(product)]
    dst_half[0] = in_half((logits[0] + logits[1] + logits[2]) * log2e, col)
    target_pair().start()

    for load in loads[5:]:
        load.wait()
    live = live_ref[0, 0]
    lane = lax.broadcasted_iota(jnp.int32, (1, BLK), 1)

    def put(slot, table):
        name = slots_ref[0, slot] + BLK * jnp.clip(slot + 1 - live, 0, 1)
        return jnp.where(lane == jnp.full((1, BLK), name, jnp.int32), slot, table)

    place_rows[...] = lax.fori_loop(0, SLOTS, put, jnp.full((1, BLK), SLOTS, jnp.int32), unroll=8)
    table = pltpu.make_async_copy(place_rows, places, local.at[9])
    table.start()
    everyone[...] = jnp.zeros(everyone.shape, jnp.float32)
    tops[SLOTS] = jnp.full((HEADS, 8, BLK), no_edge, jnp.float32)
    slot_sums[SLOTS] = jnp.zeros((HEADS, 8, BLK), jnp.float32)
    products[SLOTS] = jnp.zeros((WIDTH, BLK), jnp.float32)
    target_pair().wait_recv()
    dst[z] = dst_half[0] + dst_half[1]
    for d in range(1, ZS):
        target_z(d).start()

    for d in near_first:
        logits_y(d).wait_recv()
    for e in range(1, XS):
        logits_x(e).start()
    for d in near_first:
        feats_y(d).wait_recv()
        for e in (2, 1, 3):
            feats_x(d, e).start()
    for e in range(1, XS):
        logits_x(e).wait_recv()
    for s in range(SB):
        here, pair = s // 2, (s % 2) * 2
        everyone[8 * s : 8 * s + HEADS, :] = src_rows[pair, here] + src_rows[pair + 1, here]
    columns = everyone[...].T
    for s in range(SB):
        for h in range(HEADS):
            spread[h, s] = jnp.broadcast_to(columns[:, 8 * s + h : 8 * s + h + 1], (BLK, BLK))

    bit = jnp.left_shift(1, lax.broadcasted_iota(jnp.int32, (8, BLK), 0))

    def edges(slot, w):
        return (bits_ref[slot, pl.ds(w, 8, stride=0), :] & bit) != 0

    def slot_max(slot):
        s = slots_ref[0, slot] & (SB - 1)
        top = [jnp.full((8, BLK), no_edge, jnp.float32)] * HEADS
        for w in range(BLK // 8):
            mask = edges(slot, w)
            for h in range(HEADS):
                top[h] = jnp.maximum(top[h], jnp.where(mask, spread[h, s, 8 * w : 8 * w + 8, :], no_edge))
        for h in range(HEADS):
            tops[slot, h] = top[h]

    loop(0, SLOTS, slot_max, 2)
    table.wait()
    for d in range(1, ZS):
        target_z(d).wait_recv()

    def block_max(d):
        best = [tops[places[0, d * SB], h] for h in range(HEADS)]
        for k in range(1, SB):
            slot = places[0, d * SB + k]
            best = [jnp.maximum(best[h], tops[slot, h]) for h in range(HEADS)]
        for h in range(HEADS):
            top = jnp.max(best[h], axis=0, keepdims=True)
            maxima[d, h : h + 1, :] = jnp.where(top > -1e38, leaky(top + dst[d, h : h + 1, :]), very_low)

    loop(0, DB, block_max)

    def slot_weights(slot):
        place = slots_ref[0, slot]
        d, s = jnp.right_shift(place, 4), place & (SB - 1)
        sums = [jnp.zeros((8, BLK), jnp.float32)] * HEADS
        b = [jnp.broadcast_to(dst[d, h : h + 1, :], (8, BLK)) for h in range(HEADS)]
        m = [jnp.broadcast_to(maxima[d, h : h + 1, :], (8, BLK)) for h in range(HEADS)]
        for w in range(0, BLK // 8, 2):
            masks = [edges(slot, w), edges(slot, w + 1)]
            for h in range(HEADS):
                pair = []
                for half in range(2):
                    from_src = spread[h, s, 8 * (w + half) : 8 * (w + half) + 8, :]
                    score = leaky(from_src + b[h]) - m[h]
                    numer = jnp.where(masks[half], jnp.exp2(score), 0.0)
                    sums[h] = sums[h] + numer
                    pair.append(numer)
                weights[slot, h, 8 * w : 8 * w + 16, :] = jnp.concatenate(pair, axis=0).astype(jnp.bfloat16)
        for h in range(HEADS):
            slot_sums[slot, h] = sums[h]

    loop(0, SLOTS, slot_weights, 2)

    def block_stats(d):
        total = [slot_sums[places[0, d * SB], h] for h in range(HEADS)]
        for k in range(1, SB):
            slot = places[0, d * SB + k]
            total = [total[h] + slot_sums[slot, h] for h in range(HEADS)]
        rows = [maxima[d]] + [jnp.sum(total[h], axis=0, keepdims=True) for h in range(HEADS)]
        stats[d] = jnp.concatenate(rows, axis=0)

    loop(0, DB, block_stats)
    stats_pair().start()
    for d in range(YS):
        for e in range(1, XS):
            feats_x(d, e).wait_recv()
    eye = (
        lax.broadcasted_iota(jnp.int32, (WIDTH, WIDTH), 0) == lax.broadcasted_iota(jnp.int32, (WIDTH, WIDTH), 1)
    ).astype(jnp.bfloat16)

    def turn(s):
        block = jnp.concatenate([feats[2 * s], feats[2 * s + 1]], axis=0)
        turned[s] = lax.dot_general(eye, block, by_columns, preferred_element_type=jnp.float32).astype(jnp.bfloat16)

    for s in range(SB):
        turn(s)

    def slot_product(slot):
        s = slots_ref[0, slot] & (SB - 1)
        parts = [
            jnp.dot(turned[s, h * HD : (h + 1) * HD, :], weights[slot, h], preferred_element_type=jnp.float32)
            for h in range(HEADS)
        ]
        products[slot] = jnp.concatenate(parts, axis=0)

    loop(0, SLOTS, slot_product, 16)
    order = (4, 3, 5, 2, 6, 1, 7, 0)
    for o in order:
        d = lax.rem(z + o, ZS)

        def add(k, total):
            for i in range(4):
                total = total + products[places[0, d * SB + 4 * k + i]]
            return total

        total = lax.fori_loop(0, SB // 4, add, jnp.zeros((WIDTH, BLK), jnp.float32))
        accum[d] = total
        sent[d] = total.astype(jnp.bfloat16)
        sums_pair(d).start()
    stats_pair().wait_recv()

    def own_heads(tile):
        return jnp.where(core == 0, tile[0:2], tile[2:4]), jnp.where(core == 0, tile[4:6], tile[6:8])

    for o in order:
        d = lax.rem(z + o, ZS)
        m0, s0 = own_heads(stats[d])
        m1, s1 = own_heads(twin_stats[d])
        m = jnp.maximum(m0, m1)
        f0, f1 = jnp.exp2(m0 - m), jnp.exp2(m1 - m)
        tile = jnp.concatenate([m, s0 * f0 + s1 * f1, m, m], axis=0)
        sums_pair(d).wait_recv()
        mixed = []
        for h in range(2):
            rows = pl.ds(pl.multiple_of(core * BLK + h * HD, HD), HD)
            twin_part = twin_sent[d, h * HD : (h + 1) * HD, :].astype(jnp.float32)
            mixed.append(accum[d, rows, :] * f0[h : h + 1] + twin_part * f1[h : h + 1])
        mixed = jnp.concatenate(mixed, axis=0).astype(jnp.bfloat16)
        if o:
            joint_stats[d] = tile
            joint[d] = mixed
            stats_z(o).start()
            sums_z(o).start()
        else:
            got_stats[z] = tile
            got[z] = mixed

    for d in range(1, ZS):
        stats_z(d).wait_recv()
    every = got_stats[...]
    near = every[:, 0:2, :]
    factor = jnp.exp2(near - jnp.max(near, axis=0, keepdims=True))
    denoms = jnp.sum(factor * every[:, 2:4, :], axis=0, keepdims=True)
    factor = factor / jnp.maximum(denoms, 1.0)
    for d in range(1, ZS):
        sums_z(d).wait_recv()
    parts = []
    for h in range(2):
        part = jnp.zeros((HD, BLK), jnp.float32)
        for c in range(ZS):
            part = part + factor[c, h : h + 1, :] * got[c, h * HD : (h + 1) * HD, :].astype(jnp.float32)
        parts.append(part)
    bias = jnp.where(core == 0, bias_ref[:, :BLK], bias_ref[:, BLK:])
    blended = jnp.concatenate(parts, axis=0).T + bias
    result = jnp.where(blended > 0, blended, jnp.exp(jnp.minimum(blended, 0.0)) - 1.0).astype(jnp.bfloat16)
    half_ref[...] = jnp.where(core == 0, result[OWN:], result[:OWN])
    result_pair().start()
    out_ref[:, pl.ds(pl.multiple_of(core * BLK, BLK), BLK)] = jnp.where(core == 0, result[:OWN], result[OWN:])

    for d in range(1, YS):
        logits_y(d).wait_send()
        feats_y(d).wait_send()
    for e in range(1, XS):
        logits_x(e).wait_send()
    for d in range(YS):
        for e in range(1, XS):
            feats_x(d, e).wait_send()
    target_pair().wait_send()
    stats_pair().wait_send()
    for d in range(1, ZS):
        target_z(d).wait_send()
        stats_z(d).wait_send()
        sums_z(d).wait_send()
    loop(0, ZS, lambda d: sums_pair(d).wait_send())
    result_pair().wait()
    out_ref[:, pl.ds(pl.multiple_of((1 - core) * BLK, BLK), BLK)] = twin_half[...]


def layer(source, target, weight, score_source, score_target, bias, slots, live, bits):
    dma = pltpu.SemaphoreType.DMA
    vmem = pltpu.VMEM
    f32, bf16 = jnp.float32, jnp.bfloat16
    return pl.pallas_call(
        layer_kernel,
        out_shape=jax.ShapeDtypeStruct((OWN, WIDTH), bf16),
        in_specs=[pl.BlockSpec(memory_space=pltpu.HBM)] * 9,
        out_specs=pl.BlockSpec(memory_space=pltpu.VMEM),
        scratch_shapes=[
            vmem((OWN, WIDTH), bf16),
            vmem((OWN, WIDTH), bf16),
            vmem((WIDTH, WIDTH), bf16),
            vmem((HEADS, HD), f32),
            vmem((HEADS, HD), f32),
            vmem((1, WIDTH), f32),
            pltpu.SMEM((1, SLOTS), jnp.int32),
            pltpu.SMEM((1, 1), jnp.int32),
            vmem((SLOTS, BLK // 8, BLK), jnp.int32),
            vmem((ROWS, OWN, WIDTH), bf16),
            vmem((XS, YS, HEADS, BLK), f32),
            vmem((2, HEADS, BLK), f32),
            vmem((DB, HEADS, BLK), f32),
            vmem((1, BLK), jnp.int32),
            pltpu.SMEM((1, BLK), jnp.int32),
            vmem((BLK, BLK), f32),
            vmem((HEADS, SB, BLK, BLK), f32),
            vmem((SLOTS + 1, HEADS, 8, BLK), f32),
            vmem((DB, HEADS, BLK), f32),
            vmem((SB, WIDTH, BLK), bf16),
            vmem((SLOTS, HEADS, BLK, BLK), bf16),
            vmem((SLOTS + 1, HEADS, 8, BLK), f32),
            vmem((SLOTS + 1, WIDTH, BLK), f32),
            vmem((DB, WIDTH, BLK), f32),
            vmem((DB, WIDTH, BLK), bf16),
            vmem((DB, 8, BLK), f32),
            vmem((DB, BLK, BLK), bf16),
            vmem((DB, 8, BLK), f32),
            vmem((DB, BLK, BLK), bf16),
            vmem((DB, 8, BLK), f32),
            vmem((DB, BLK, BLK), bf16),
            vmem((DB, 8, BLK), f32),
            vmem((OWN, BLK), bf16),
            vmem((OWN, BLK), bf16),
            dma((10,)),
            dma((YS,)), dma((YS,)),
            dma((XS,)), dma((XS,)),
            dma((ZS,)), dma((ZS,)),
            dma((YS,)), dma((YS,)),
            dma((YS, XS)), dma((YS, XS)),
            dma((ZS,)), dma((ZS,)),
            dma((ZS,)), dma((ZS,)),
            dma((ZS,)), dma((ZS,)),
            dma((3,)), dma((3,)),
        ],
        compiler_params=pltpu.CompilerParams(collective_id=0, has_side_effects=True, vmem_limit_bytes=60 << 20),
        name="layer",
    )(source, target, weight, score_source, score_target, bias, slots, live, bits)


def body(
    source_features, target_features, weight, score_source, score_target, out_bias,
    block_list, block_count, edge_bits,
):
    return layer(
        source_features[0], target_features, weight, score_source, score_target, out_bias.reshape(1, WIDTH),
        block_list[0], block_count, edge_bits[0, 0],
    )


def solution(mesh):
    placed = (
        P("col", "row", None),
        P(("row", "col"), None),
        P(),
        P(),
        P(),
        P(),
        P("row", "col", None),
        P("row", "col"),
        P("row", "col", None, None, None),
    )
    return jax.shard_map(
        body, mesh=mesh, in_specs=placed, out_specs=P(("row", "col"), None), check_vma=False
    )
```

```python
import jax
import jax.numpy as jnp
from jax import lax
from jax.experimental import pallas as pl
from jax.experimental.pallas import tpu as pltpu
from jax.sharding import PartitionSpec as P

BLK = 128
SB = 16
DB = 8
SLOTS = 48
HEADS = 4
HD = 64
WIDTH = 256
ROWS = 32
COLS = 16
XS = 4
YS = 8
ZS = 8
OWN = 64

very_low = -1e30
no_edge = -3e38
slope = 0.2
log2e = 1.4426950408889634
MESH = pl.DeviceIdType.MESH
by_columns = (((1,), (1,)), ((), ()))


def in_three(x):
    high = x.astype(jnp.bfloat16)
    rest = x - high.astype(jnp.float32)
    middle = rest.astype(jnp.bfloat16)
    low = (rest - middle.astype(jnp.float32)).astype(jnp.bfloat16)
    return low, middle, high


def leaky(x):
    return jnp.maximum(x, slope * x)


def loop(first, last, step, unroll=1):
    def one(i, _):
        step(i)
        return 0

    lax.fori_loop(first, last, one, 0, unroll=unroll)


def in_half(rows, position):
    twice = jnp.concatenate([rows, rows], axis=1)
    half = lax.broadcasted_iota(jnp.int32, (HEADS, BLK), 1) // OWN
    return jnp.where(half == lax.rem(position, 2), twice[:HEADS], 0.0)


def flat_scores(ref):
    return jnp.concatenate([ref[h : h + 1, :] for h in range(HEADS)], axis=1)


def layer_kernel(
    src_hbm, tgt_hbm, weight_hbm, source_hbm, target_hbm, bias_hbm, slots_hbm, live_hbm, bits_hbm,
    out_ref,
    src_ref, tgt_ref, weight_ref, source_ref, target_ref, bias_ref, slots_ref, live_ref, bits_ref,
    feats, src_rows, dst_half, dst, place_rows, places, everyone, spread, tops, maxima, turned,
    weights, slot_sums, products, accum, sent, stats, twin_sent, twin_stats,
    joint, joint_stats, got, got_stats, half_ref, kept_half,
    local, send_ay, recv_ay, send_ax, recv_ax, send_b, recv_b, send_y, recv_y, send_x, recv_x,
    send_p, recv_p, send_j, recv_j, send_k, recv_k, send_one, recv_one,
):
    row, col = lax.axis_index("row"), lax.axis_index("col")
    x, y = lax.rem(row, XS), row // XS
    z, core = col // 2, lax.rem(col, 2)
    twin = (row, col + 1 - 2 * core)
    pairs = (
        (weight_hbm, weight_ref), (src_hbm, src_ref), (source_hbm, source_ref), (tgt_hbm, tgt_ref),
        (target_hbm, target_ref), (slots_hbm, slots_ref), (live_hbm, live_ref), (bits_hbm, bits_ref),
        (bias_hbm, bias_ref),
    )
    loads = [pltpu.make_async_copy(a, b, local.at[i]) for i, (a, b) in enumerate(pairs)]
    for load in loads:
        load.start()

    def at_x(d):
        return (y * XS + lax.rem(x + d, XS), col)

    def at_y(d):
        return (lax.rem(y + d, YS) * XS + x, col)

    def at_z(d):
        return (row, lax.rem(z + d, ZS) * 2 + core)

    barrier = pltpu.get_barrier_semaphore()
    for d in range(1, YS):
        pl.semaphore_signal(barrier, inc=1, device_id=at_y(d), device_id_type=MESH)
    for d in range(1, XS):
        pl.semaphore_signal(barrier, inc=1, device_id=at_x(d), device_id_type=MESH)
    for d in range(1, ZS):
        pl.semaphore_signal(barrier, inc=1, device_id=at_z(d), device_id_type=MESH)
    pl.semaphore_signal(barrier, inc=1, device_id=twin, device_id_type=MESH)

    def send(source, target, semaphores, device):
        return pltpu.make_async_remote_copy(
            src_ref=source, dst_ref=target, send_sem=semaphores[0], recv_sem=semaphores[1],
            device_id=device, device_id_type=MESH,
        )

    def logits_y(d):
        return send(src_rows.at[x, y], src_rows.at[x, y], (send_ay.at[d], recv_ay.at[d]), at_y(d))

    def logits_x(d):
        return send(src_rows.at[x], src_rows.at[x], (send_ax.at[d], recv_ax.at[d]), at_x(d))

    def feats_y(d):
        return send(feats.at[row], feats.at[row], (send_y.at[d], recv_y.at[d]), at_y(d))

    def feats_x(d, e):
        block = lax.rem(y - d + YS, YS) * XS + x
        return send(feats.at[block], feats.at[block], (send_x.at[d, e], recv_x.at[d, e]), at_x(e))

    def target_pair():
        return send(dst_half.at[0], dst_half.at[1], (send_one.at[0], recv_one.at[0]), twin)

    def target_z(d):
        return send(dst.at[z], dst.at[z], (send_b.at[d], recv_b.at[d]), at_z(d))

    def stats_pair():
        return send(stats, twin_stats, (send_one.at[1], recv_one.at[1]), twin)

    def sums_pair(d):
        theirs = pl.ds(pl.multiple_of((1 - core) * BLK, BLK), BLK)
        return send(sent.at[d, theirs], twin_sent.at[d], (send_p.at[d], recv_p.at[d]), twin)

    def sums_z(d):
        return send(joint.at[lax.rem(z + d, ZS)], got.at[z], (send_j.at[d], recv_j.at[d]), at_z(d))

    def stats_z(d):
        return send(joint_stats.at[lax.rem(z + d, ZS)], got_stats.at[z], (send_k.at[d], recv_k.at[d]), at_z(d))

    def result_pair():
        here = out_ref.at[:, pl.ds(pl.multiple_of(core * BLK, BLK), BLK)]
        return send(half_ref, here, (send_one.at[2], recv_one.at[2]), twin)

    for load in loads[:3]:
        load.wait()
    own = jnp.dot(src_ref[...], weight_ref[...], preferred_element_type=jnp.float32).astype(jnp.bfloat16)
    feats[row] = own
    head_of = lax.broadcasted_iota(jnp.int32, (8, WIDTH), 1) // HD
    pick = head_of == lax.broadcasted_iota(jnp.int32, (8, WIDTH), 0)
    parts = jnp.concatenate(in_three(jnp.where(pick, flat_scores(source_ref), 0.0)), axis=0)
    logits = lax.dot_general(parts, own, by_columns, preferred_element_type=jnp.float32)
    src_rows[x, y] = in_half((logits[0:8] + logits[8:16] + logits[16:24]) * log2e, row)
    pl.semaphore_wait(barrier, XS + YS + ZS - 2)

    far_first = (4, 3, 5, 2, 6, 1, 7)
    near_first = (1, 7, 2, 6, 3, 5, 4)
    for d in far_first:
        logits_y(d).start()
    for e in (2, 1, 3):
        feats_x(0, e).start()
    for d in near_first:
        feats_y(d).start()

    for load in loads[3:5]:
        load.wait()
    product = jnp.dot(tgt_ref[...], weight_ref[...], preferred_element_type=jnp.float32) * flat_scores(target_ref)
    ones = pick.astype(jnp.bfloat16)
    logits = [lax.dot_general(ones, part, by_columns, preferred_element_type=jnp.float32) for part in in_three(product)]
    dst_half[0] = in_half((logits[0] + logits[1] + logits[2]) * log2e, col)
    target_pair().start()

    for load in loads[5:]:
        load.wait()
    live = live_ref[0, 0]
    lane = lax.broadcasted_iota(jnp.int32, (1, BLK), 1)

    def put(slot, table):
        name = slots_ref[0, slot] + BLK * jnp.clip(slot + 1 - live, 0, 1)
        return jnp.where(lane == jnp.full((1, BLK), name, jnp.int32), slot, table)

    place_rows[...] = lax.fori_loop(0, SLOTS, put, jnp.full((1, BLK), SLOTS, jnp.int32), unroll=8)
    table = pltpu.make_async_copy(place_rows, places, local.at[9])
    table.start()
    everyone[...] = jnp.zeros(everyone.shape, jnp.float32)
    tops[SLOTS] = jnp.full((HEADS, 8, BLK), no_edge, jnp.float32)
    slot_sums[SLOTS] = jnp.zeros((HEADS, 8, BLK), jnp.float32)
    products[SLOTS] = jnp.zeros((WIDTH, BLK), jnp.float32)
    target_pair().wait_recv()
    dst[z] = dst_half[0] + dst_half[1]
    for d in range(1, ZS):
        target_z(d).start()

    for d in near_first:
        logits_y(d).wait_recv()
    for e in range(1, XS):
        logits_x(e).start()
    for d in near_first:
        feats_y(d).wait_recv()
        for e in (2, 1, 3):
            feats_x(d, e).start()
    for e in range(1, XS):
        logits_x(e).wait_recv()
    for s in range(SB):
        here, pair = s // 2, (s % 2) * 2
        everyone[8 * s : 8 * s + HEADS, :] = src_rows[pair, here] + src_rows[pair + 1, here]
    columns = everyone[...].T
    for s in range(SB):
        for h in range(HEADS):
            spread[h, s] = jnp.broadcast_to(columns[:, 8 * s + h : 8 * s + h + 1], (BLK, BLK))

    bit = jnp.left_shift(1, lax.broadcasted_iota(jnp.int32, (8, BLK), 0))

    def edges(slot, w):
        return (bits_ref[slot, pl.ds(w, 8, stride=0), :] & bit) != 0

    def slot_max(slot):
        s = slots_ref[0, slot] & (SB - 1)
        top = [jnp.full((8, BLK), no_edge, jnp.float32)] * HEADS
        for w in range(BLK // 8):
            mask = edges(slot, w)
            for h in range(HEADS):
                top[h] = jnp.maximum(top[h], jnp.where(mask, spread[h, s, 8 * w : 8 * w + 8, :], no_edge))
        for h in range(HEADS):
            tops[slot, h] = top[h]

    loop(0, SLOTS, slot_max, 2)
    table.wait()
    for d in range(1, ZS):
        target_z(d).wait_recv()

    def block_max(d):
        best = [tops[places[0, d * SB], h] for h in range(HEADS)]
        for k in range(1, SB):
            slot = places[0, d * SB + k]
            best = [jnp.maximum(best[h], tops[slot, h]) for h in range(HEADS)]
        for h in range(HEADS):
            top = jnp.max(best[h], axis=0, keepdims=True)
            maxima[d, h : h + 1, :] = jnp.where(top > -1e38, leaky(top + dst[d, h : h + 1, :]), very_low)

    loop(0, DB, block_max)

    def slot_weights(slot):
        place = slots_ref[0, slot]
        d, s = jnp.right_shift(place, 4), place & (SB - 1)
        sums = [jnp.zeros((8, BLK), jnp.float32)] * HEADS
        b = [jnp.broadcast_to(dst[d, h : h + 1, :], (8, BLK)) for h in range(HEADS)]
        m = [jnp.broadcast_to(maxima[d, h : h + 1, :], (8, BLK)) for h in range(HEADS)]
        for w in range(0, BLK // 8, 2):
            masks = [edges(slot, w), edges(slot, w + 1)]
            for h in range(HEADS):
                pair = []
                for half in range(2):
                    from_src = spread[h, s, 8 * (w + half) : 8 * (w + half) + 8, :]
                    score = leaky(from_src + b[h]) - m[h]
                    numer = jnp.where(masks[half], jnp.exp2(score), 0.0)
                    sums[h] = sums[h] + numer
                    pair.append(numer)
                weights[slot, h, 8 * w : 8 * w + 16, :] = jnp.concatenate(pair, axis=0).astype(jnp.bfloat16)
        for h in range(HEADS):
            slot_sums[slot, h] = sums[h]

    loop(0, SLOTS, slot_weights, 2)

    def block_stats(d):
        total = [slot_sums[places[0, d * SB], h] for h in range(HEADS)]
        for k in range(1, SB):
            slot = places[0, d * SB + k]
            total = [total[h] + slot_sums[slot, h] for h in range(HEADS)]
        rows = [maxima[d]] + [jnp.sum(total[h], axis=0, keepdims=True) for h in range(HEADS)]
        stats[d] = jnp.concatenate(rows, axis=0)

    loop(0, DB, block_stats)
    stats_pair().start()
    for d in range(YS):
        for e in range(1, XS):
            feats_x(d, e).wait_recv()
    eye = (
        lax.broadcasted_iota(jnp.int32, (WIDTH, WIDTH), 0) == lax.broadcasted_iota(jnp.int32, (WIDTH, WIDTH), 1)
    ).astype(jnp.bfloat16)

    def turn(s):
        block = jnp.concatenate([feats[2 * s], feats[2 * s + 1]], axis=0)
        turned[s] = lax.dot_general(eye, block, by_columns, preferred_element_type=jnp.float32).astype(jnp.bfloat16)

    for s in range(SB):
        turn(s)

    def slot_product(slot):
        s = slots_ref[0, slot] & (SB - 1)
        parts = [
            jnp.dot(turned[s, h * HD : (h + 1) * HD, :], weights[slot, h], preferred_element_type=jnp.float32)
            for h in range(HEADS)
        ]
        products[slot] = jnp.concatenate(parts, axis=0)

    loop(0, SLOTS, slot_product, 16)
    order = (4, 3, 5, 2, 6, 1, 7, 0)
    for o in order:
        d = lax.rem(z + o, ZS)

        def add(k, total):
            for i in range(4):
                total = total + products[places[0, d * SB + 4 * k + i]]
            return total

        total = lax.fori_loop(0, SB // 4, add, jnp.zeros((WIDTH, BLK), jnp.float32))
        accum[d] = total
        sent[d] = total.astype(jnp.bfloat16)
        sums_pair(d).start()
    stats_pair().wait_recv()

    def own_heads(tile):
        return jnp.where(core == 0, tile[0:2], tile[2:4]), jnp.where(core == 0, tile[4:6], tile[6:8])

    for o in order:
        d = lax.rem(z + o, ZS)
        m0, s0 = own_heads(stats[d])
        m1, s1 = own_heads(twin_stats[d])
        m = jnp.maximum(m0, m1)
        f0, f1 = jnp.exp2(m0 - m), jnp.exp2(m1 - m)
        tile = jnp.concatenate([m, s0 * f0 + s1 * f1, m, m], axis=0)
        sums_pair(d).wait_recv()
        mixed = []
        for h in range(2):
            rows = pl.ds(pl.multiple_of(core * BLK + h * HD, HD), HD)
            twin_part = twin_sent[d, h * HD : (h + 1) * HD, :].astype(jnp.float32)
            mixed.append(accum[d, rows, :] * f0[h : h + 1] + twin_part * f1[h : h + 1])
        mixed = jnp.concatenate(mixed, axis=0).astype(jnp.bfloat16)
        if o:
            joint_stats[d] = tile
            joint[d] = mixed
            stats_z(o).start()
            sums_z(o).start()
        else:
            got_stats[z] = tile
            got[z] = mixed

    for d in range(1, ZS):
        stats_z(d).wait_recv()
    every = got_stats[...]
    near = every[:, 0:2, :]
    factor = jnp.exp2(near - jnp.max(near, axis=0, keepdims=True))
    denoms = jnp.sum(factor * every[:, 2:4, :], axis=0, keepdims=True)
    factor = factor / jnp.maximum(denoms, 1.0)
    for d in range(1, ZS):
        sums_z(d).wait_recv()
    parts = []
    for h in range(2):
        part = jnp.zeros((HD, BLK), jnp.float32)
        for c in range(ZS):
            part = part + factor[c, h : h + 1, :] * got[c, h * HD : (h + 1) * HD, :].astype(jnp.float32)
        parts.append(part)
    bias = jnp.where(core == 0, bias_ref[:, :BLK], bias_ref[:, BLK:])
    blended = jnp.concatenate(parts, axis=0).T + bias
    result = jnp.where(blended > 0, blended, jnp.exp(jnp.minimum(blended, 0.0)) - 1.0).astype(jnp.bfloat16)
    half_ref[...] = jnp.where(core == 0, result[OWN:], result[:OWN])
    result_pair().start()
    kept_half[...] = jnp.where(core == 0, result[:OWN], result[OWN:])
    keep = pltpu.make_async_copy(kept_half, out_ref.at[:, pl.ds(pl.multiple_of(core * BLK, BLK), BLK)], local.at[10])
    keep.start()

    for d in range(1, YS):
        logits_y(d).wait_send()
        feats_y(d).wait_send()
    for e in range(1, XS):
        logits_x(e).wait_send()
    for d in range(YS):
        for e in range(1, XS):
            feats_x(d, e).wait_send()
    target_pair().wait_send()
    stats_pair().wait_send()
    for d in range(1, ZS):
        target_z(d).wait_send()
        stats_z(d).wait_send()
        sums_z(d).wait_send()
    loop(0, ZS, lambda d: sums_pair(d).wait_send())
    keep.wait()
    result_pair().wait()


def layer(source, target, weight, score_source, score_target, bias, slots, live, bits):
    dma = pltpu.SemaphoreType.DMA
    vmem = pltpu.VMEM
    f32, bf16 = jnp.float32, jnp.bfloat16
    return pl.pallas_call(
        layer_kernel,
        out_shape=pltpu.VMEM((OWN, WIDTH), bf16),
        in_specs=[pl.BlockSpec(memory_space=pltpu.HBM)] * 9,
        out_specs=pl.BlockSpec(memory_space=pltpu.VMEM),
        scratch_shapes=[
            vmem((OWN, WIDTH), bf16),
            vmem((OWN, WIDTH), bf16),
            vmem((WIDTH, WIDTH), bf16),
            vmem((HEADS, HD), f32),
            vmem((HEADS, HD), f32),
            vmem((1, WIDTH), f32),
            pltpu.SMEM((1, SLOTS), jnp.int32),
            pltpu.SMEM((1, 1), jnp.int32),
            vmem((SLOTS, BLK // 8, BLK), jnp.int32),
            vmem((ROWS, OWN, WIDTH), bf16),
            vmem((XS, YS, HEADS, BLK), f32),
            vmem((2, HEADS, BLK), f32),
            vmem((DB, HEADS, BLK), f32),
            vmem((1, BLK), jnp.int32),
            pltpu.SMEM((1, BLK), jnp.int32),
            vmem((BLK, BLK), f32),
            vmem((HEADS, SB, BLK, BLK), f32),
            vmem((SLOTS + 1, HEADS, 8, BLK), f32),
            vmem((DB, HEADS, BLK), f32),
            vmem((SB, WIDTH, BLK), bf16),
            vmem((SLOTS, HEADS, BLK, BLK), bf16),
            vmem((SLOTS + 1, HEADS, 8, BLK), f32),
            vmem((SLOTS + 1, WIDTH, BLK), f32),
            vmem((DB, WIDTH, BLK), f32),
            vmem((DB, WIDTH, BLK), bf16),
            vmem((DB, 8, BLK), f32),
            vmem((DB, BLK, BLK), bf16),
            vmem((DB, 8, BLK), f32),
            vmem((DB, BLK, BLK), bf16),
            vmem((DB, 8, BLK), f32),
            vmem((DB, BLK, BLK), bf16),
            vmem((DB, 8, BLK), f32),
            vmem((OWN, BLK), bf16),
            vmem((OWN, BLK), bf16),
            dma((11,)),
            dma((YS,)), dma((YS,)),
            dma((XS,)), dma((XS,)),
            dma((ZS,)), dma((ZS,)),
            dma((YS,)), dma((YS,)),
            dma((YS, XS)), dma((YS, XS)),
            dma((ZS,)), dma((ZS,)),
            dma((ZS,)), dma((ZS,)),
            dma((ZS,)), dma((ZS,)),
            dma((3,)), dma((3,)),
        ],
        compiler_params=pltpu.CompilerParams(collective_id=0, has_side_effects=True, vmem_limit_bytes=60 << 20),
        name="layer",
    )(source, target, weight, score_source, score_target, bias, slots, live, bits)


def body(
    source_features, target_features, weight, score_source, score_target, out_bias,
    block_list, block_count, edge_bits,
):
    return layer(
        source_features[0], target_features, weight, score_source, score_target, out_bias.reshape(1, WIDTH),
        block_list[0], block_count, edge_bits[0, 0],
    )


def solution(mesh):
    placed = (
        P("col", "row", None),
        P(("row", "col"), None),
        P(),
        P(),
        P(),
        P(),
        P("row", "col", None),
        P("row", "col"),
        P("row", "col", None, None, None),
    )
    return jax.shard_map(
        body, mesh=mesh, in_specs=placed, out_specs=P(("row", "col"), None), check_vma=False
    )
```

```python
import jax
import jax.numpy as jnp
from jax import lax
from jax.experimental import pallas as pl
from jax.experimental.pallas import tpu as pltpu
from jax.sharding import PartitionSpec as P

BLK = 128
SB = 16
DB = 8
SLOTS = 48
HEADS = 4
HD = 64
WIDTH = 256
ROWS = 32
COLS = 16
XS = 4
YS = 8
ZS = 8
OWN = 64

very_low = -1e30
no_edge = -3e38
slope = 0.2
log2e = 1.4426950408889634
MESH = pl.DeviceIdType.MESH
by_columns = (((1,), (1,)), ((), ()))


def in_three(x):
    high = x.astype(jnp.bfloat16)
    rest = x - high.astype(jnp.float32)
    middle = rest.astype(jnp.bfloat16)
    low = (rest - middle.astype(jnp.float32)).astype(jnp.bfloat16)
    return low, middle, high


def leaky(x):
    return jnp.maximum(x, slope * x)


def loop(first, last, step, unroll=1):
    def one(i, _):
        step(i)
        return 0

    lax.fori_loop(first, last, one, 0, unroll=unroll)


def in_half(rows, position):
    twice = jnp.concatenate([rows, rows], axis=1)
    half = lax.broadcasted_iota(jnp.int32, (HEADS, BLK), 1) // OWN
    return jnp.where(half == lax.rem(position, 2), twice[:HEADS], 0.0)


def flat_scores(ref):
    return jnp.concatenate([ref[h : h + 1, :] for h in range(HEADS)], axis=1)


def layer_kernel(
    src_hbm, tgt_hbm, weight_hbm, source_hbm, target_hbm, bias_hbm, slots_hbm, live_hbm, bits_hbm,
    out_ref,
    src_ref, tgt_ref, weight_ref, source_ref, target_ref, bias_ref, slots_ref, live_ref, bits_ref,
    feats, src_rows, dst_half, dst, place_rows, places, everyone, spread, tops, maxima, turned,
    weights, slot_sums, products, accum, sent, stats, twin_sent, twin_stats,
    joint, joint_stats, got, got_stats, half_ref, kept_half,
    local, send_ay, recv_ay, send_ax, recv_ax, send_b, recv_b, send_y, recv_y, send_x, recv_x,
    send_p, recv_p, send_j, recv_j, send_k, recv_k, send_one, recv_one,
):
    row, col = lax.axis_index("row"), lax.axis_index("col")
    x, y = lax.rem(row, XS), row // XS
    z, core = col // 2, lax.rem(col, 2)
    twin = (row, col + 1 - 2 * core)
    pairs = (
        (weight_hbm, weight_ref), (src_hbm, src_ref), (source_hbm, source_ref), (tgt_hbm, tgt_ref),
        (target_hbm, target_ref), (slots_hbm, slots_ref), (live_hbm, live_ref), (bits_hbm, bits_ref),
        (bias_hbm, bias_ref),
    )
    loads = [pltpu.make_async_copy(a, b, local.at[i]) for i, (a, b) in enumerate(pairs)]
    for load in loads:
        load.start()

    def at_x(d):
        return (y * XS + lax.rem(x + d, XS), col)

    def at_y(d):
        return (lax.rem(y + d, YS) * XS + x, col)

    def at_z(d):
        return (row, lax.rem(z + d, ZS) * 2 + core)

    barrier = pltpu.get_barrier_semaphore()
    for d in range(1, YS):
        pl.semaphore_signal(barrier, inc=1, device_id=at_y(d), device_id_type=MESH)
    for d in range(1, XS):
        pl.semaphore_signal(barrier, inc=1, device_id=at_x(d), device_id_type=MESH)
    for d in range(1, ZS):
        pl.semaphore_signal(barrier, inc=1, device_id=at_z(d), device_id_type=MESH)
    pl.semaphore_signal(barrier, inc=1, device_id=twin, device_id_type=MESH)

    def send(source, target, semaphores, device):
        return pltpu.make_async_remote_copy(
            src_ref=source, dst_ref=target, send_sem=semaphores[0], recv_sem=semaphores[1],
            device_id=device, device_id_type=MESH,
        )

    def logits_y(d):
        return send(src_rows.at[x, y], src_rows.at[x, y], (send_ay.at[d], recv_ay.at[d]), at_y(d))

    def logits_x(d):
        return send(src_rows.at[x], src_rows.at[x], (send_ax.at[d], recv_ax.at[d]), at_x(d))

    def feats_y(d):
        return send(feats.at[row], feats.at[row], (send_y.at[d], recv_y.at[d]), at_y(d))

    def feats_x(d, e):
        block = lax.rem(y - d + YS, YS) * XS + x
        return send(feats.at[block], feats.at[block], (send_x.at[d, e], recv_x.at[d, e]), at_x(e))

    def target_pair():
        return send(dst_half.at[0], dst_half.at[1], (send_one.at[0], recv_one.at[0]), twin)

    def target_z(d):
        return send(dst.at[z], dst.at[z], (send_b.at[d], recv_b.at[d]), at_z(d))

    def stats_pair():
        return send(stats, twin_stats, (send_one.at[1], recv_one.at[1]), twin)

    def sums_pair(d):
        theirs = pl.ds(pl.multiple_of((1 - core) * BLK, BLK), BLK)
        return send(sent.at[d, theirs], twin_sent.at[d], (send_p.at[d], recv_p.at[d]), twin)

    def sums_z(d):
        return send(joint.at[lax.rem(z + d, ZS)], got.at[z], (send_j.at[d], recv_j.at[d]), at_z(d))

    def stats_z(d):
        return send(joint_stats.at[lax.rem(z + d, ZS)], got_stats.at[z], (send_k.at[d], recv_k.at[d]), at_z(d))

    def result_pair():
        here = out_ref.at[:, pl.ds(pl.multiple_of(core * BLK, BLK), BLK)]
        return send(half_ref, here, (send_one.at[2], recv_one.at[2]), twin)

    for load in loads[:3]:
        load.wait()
    own = jnp.dot(src_ref[...], weight_ref[...], preferred_element_type=jnp.float32).astype(jnp.bfloat16)
    feats[row] = own
    head_of = lax.broadcasted_iota(jnp.int32, (8, WIDTH), 1) // HD
    pick = head_of == lax.broadcasted_iota(jnp.int32, (8, WIDTH), 0)
    parts = jnp.concatenate(in_three(jnp.where(pick, flat_scores(source_ref), 0.0)), axis=0)
    logits = lax.dot_general(parts, own, by_columns, preferred_element_type=jnp.float32)
    src_rows[x, y] = in_half((logits[0:8] + logits[8:16] + logits[16:24]) * log2e, row)
    pl.semaphore_wait(barrier, XS + YS + ZS - 2)

    far_first = (4, 3, 5, 2, 6, 1, 7)
    near_first = (1, 7, 2, 6, 3, 5, 4)
    for d in far_first:
        logits_y(d).start()
    for e in (2, 1, 3):
        feats_x(0, e).start()
    for d in near_first:
        feats_y(d).start()

    for load in loads[3:5]:
        load.wait()
    product = jnp.dot(tgt_ref[...], weight_ref[...], preferred_element_type=jnp.float32) * flat_scores(target_ref)
    ones = pick.astype(jnp.bfloat16)
    logits = [lax.dot_general(ones, part, by_columns, preferred_element_type=jnp.float32) for part in in_three(product)]
    dst_half[0] = in_half((logits[0] + logits[1] + logits[2]) * log2e, col)
    target_pair().start()

    for load in loads[5:]:
        load.wait()
    live = live_ref[0, 0]
    lane = lax.broadcasted_iota(jnp.int32, (1, BLK), 1)

    def put(slot, table):
        name = slots_ref[0, slot] + BLK * jnp.clip(slot + 1 - live, 0, 1)
        return jnp.where(lane == jnp.full((1, BLK), name, jnp.int32), slot, table)

    place_rows[...] = lax.fori_loop(0, SLOTS, put, jnp.full((1, BLK), SLOTS, jnp.int32), unroll=8)
    table = pltpu.make_async_copy(place_rows, places, local.at[9])
    table.start()
    everyone[...] = jnp.zeros(everyone.shape, jnp.float32)
    tops[SLOTS] = jnp.full((HEADS, 8, BLK), no_edge, jnp.float32)
    slot_sums[SLOTS] = jnp.zeros((HEADS, 8, BLK), jnp.float32)
    products[SLOTS] = jnp.zeros((WIDTH, BLK), jnp.float32)
    target_pair().wait_recv()
    dst[z] = dst_half[0] + dst_half[1]
    for d in range(1, ZS):
        target_z(d).start()

    for d in near_first:
        logits_y(d).wait_recv()
    for e in range(1, XS):
        logits_x(e).start()
    for d in near_first:
        feats_y(d).wait_recv()
        for e in (2, 1, 3):
            feats_x(d, e).start()
    for e in range(1, XS):
        logits_x(e).wait_recv()
    for s in range(SB):
        here, pair = s // 2, (s % 2) * 2
        everyone[8 * s : 8 * s + HEADS, :] = src_rows[pair, here] + src_rows[pair + 1, here]
    columns = everyone[...].T
    for s in range(SB):
        for h in range(HEADS):
            spread[h, s] = jnp.broadcast_to(columns[:, 8 * s + h : 8 * s + h + 1], (BLK, BLK))

    bit = jnp.left_shift(1, lax.broadcasted_iota(jnp.int32, (8, BLK), 0))

    def edges(slot, w):
        return (bits_ref[slot, pl.ds(w, 8, stride=0), :] & bit) != 0

    def slot_max(slot):
        s = slots_ref[0, slot] & (SB - 1)
        top = [jnp.full((8, BLK), no_edge, jnp.float32)] * HEADS
        for w in range(BLK // 8):
            mask = edges(slot, w)
            for h in range(HEADS):
                top[h] = jnp.maximum(top[h], jnp.where(mask, spread[h, s, 8 * w : 8 * w + 8, :], no_edge))
        for h in range(HEADS):
            tops[slot, h] = top[h]

    loop(0, SLOTS, slot_max, 2)
    table.wait()
    for d in range(1, ZS):
        target_z(d).wait_recv()

    def block_max(d):
        best = [tops[places[0, d * SB], h] for h in range(HEADS)]
        for k in range(1, SB):
            slot = places[0, d * SB + k]
            best = [jnp.maximum(best[h], tops[slot, h]) for h in range(HEADS)]
        for h in range(HEADS):
            top = jnp.max(best[h], axis=0, keepdims=True)
            maxima[d, h : h + 1, :] = jnp.where(top > -1e38, leaky(top + dst[d, h : h + 1, :]), very_low)

    loop(0, DB, block_max)

    def slot_weights(slot):
        place = slots_ref[0, slot]
        d, s = jnp.right_shift(place, 4), place & (SB - 1)
        sums = [jnp.zeros((8, BLK), jnp.float32)] * HEADS
        b = [jnp.broadcast_to(dst[d, h : h + 1, :], (8, BLK)) for h in range(HEADS)]
        m = [jnp.broadcast_to(maxima[d, h : h + 1, :], (8, BLK)) for h in range(HEADS)]
        for w in range(0, BLK // 8, 2):
            masks = [edges(slot, w), edges(slot, w + 1)]
            for h in range(HEADS):
                pair = []
                for half in range(2):
                    from_src = spread[h, s, 8 * (w + half) : 8 * (w + half) + 8, :]
                    score = leaky(from_src + b[h]) - m[h]
                    numer = jnp.where(masks[half], jnp.exp2(score), 0.0)
                    sums[h] = sums[h] + numer
                    pair.append(numer)
                weights[slot, h, 8 * w : 8 * w + 16, :] = jnp.concatenate(pair, axis=0).astype(jnp.bfloat16)
        for h in range(HEADS):
            slot_sums[slot, h] = sums[h]

    loop(0, SLOTS, slot_weights, 2)

    def block_stats(d):
        total = [slot_sums[places[0, d * SB], h] for h in range(HEADS)]
        for k in range(1, SB):
            slot = places[0, d * SB + k]
            total = [total[h] + slot_sums[slot, h] for h in range(HEADS)]
        rows = [maxima[d]] + [jnp.sum(total[h], axis=0, keepdims=True) for h in range(HEADS)]
        stats[d] = jnp.concatenate(rows, axis=0)

    loop(0, DB, block_stats)
    stats_pair().start()
    for d in range(YS):
        for e in range(1, XS):
            feats_x(d, e).wait_recv()
    eye = (
        lax.broadcasted_iota(jnp.int32, (WIDTH, WIDTH), 0) == lax.broadcasted_iota(jnp.int32, (WIDTH, WIDTH), 1)
    ).astype(jnp.bfloat16)

    def turn(s):
        block = jnp.concatenate([feats[2 * s], feats[2 * s + 1]], axis=0)
        turned[s] = lax.dot_general(eye, block, by_columns, preferred_element_type=jnp.float32).astype(jnp.bfloat16)

    for s in range(SB):
        turn(s)

    def slot_product(slot):
        s = slots_ref[0, slot] & (SB - 1)
        parts = [
            jnp.dot(turned[s, h * HD : (h + 1) * HD, :], weights[slot, h], preferred_element_type=jnp.float32)
            for h in range(HEADS)
        ]
        products[slot] = jnp.concatenate(parts, axis=0)

    loop(0, SLOTS, slot_product, 16)
    order = (4, 3, 5, 2, 6, 1, 7, 0)
    for o in order:
        d = lax.rem(z + o, ZS)

        def add(k, total):
            for i in range(4):
                total = total + products[places[0, d * SB + 4 * k + i]]
            return total

        total = lax.fori_loop(0, SB // 4, add, jnp.zeros((WIDTH, BLK), jnp.float32))
        accum[d] = total
        sent[d] = total.astype(jnp.bfloat16)
        sums_pair(d).start()
    stats_pair().wait_recv()

    def own_heads(tile):
        return jnp.where(core == 0, tile[0:2], tile[2:4]), jnp.where(core == 0, tile[4:6], tile[6:8])

    for o in order:
        d = lax.rem(z + o, ZS)
        m0, s0 = own_heads(stats[d])
        m1, s1 = own_heads(twin_stats[d])
        m = jnp.maximum(m0, m1)
        f0, f1 = jnp.exp2(m0 - m), jnp.exp2(m1 - m)
        tile = jnp.concatenate([m, s0 * f0 + s1 * f1, m, m], axis=0)
        sums_pair(d).wait_recv()
        mixed = []
        for h in range(2):
            rows = pl.ds(pl.multiple_of(core * BLK + h * HD, HD), HD)
            twin_part = twin_sent[d, h * HD : (h + 1) * HD, :].astype(jnp.float32)
            mixed.append(accum[d, rows, :] * f0[h : h + 1] + twin_part * f1[h : h + 1])
        mixed = jnp.concatenate(mixed, axis=0).astype(jnp.bfloat16)
        if o:
            joint_stats[d] = tile
            joint[d] = mixed
            stats_z(o).start()
            sums_z(o).start()
        else:
            got_stats[z] = tile
            got[z] = mixed

    for d in range(1, YS):
        logits_y(d).wait_send()
        feats_y(d).wait_send()
    for e in range(1, XS):
        logits_x(e).wait_send()
    for d in range(YS):
        for e in range(1, XS):
            feats_x(d, e).wait_send()
    target_pair().wait_send()
    stats_pair().wait_send()
    for d in range(1, ZS):
        target_z(d).wait_send()
    loop(0, ZS, lambda d: sums_pair(d).wait_send())

    for d in range(1, ZS):
        stats_z(d).wait_recv()
    every = got_stats[...]
    near = every[:, 0:2, :]
    factor = jnp.exp2(near - jnp.max(near, axis=0, keepdims=True))
    denoms = jnp.sum(factor * every[:, 2:4, :], axis=0, keepdims=True)
    factor = factor / jnp.maximum(denoms, 1.0)
    for d in range(1, ZS):
        sums_z(d).wait_recv()
    parts = []
    for h in range(2):
        part = jnp.zeros((HD, BLK), jnp.float32)
        for c in range(ZS):
            part = part + factor[c, h : h + 1, :] * got[c, h * HD : (h + 1) * HD, :].astype(jnp.float32)
        parts.append(part)
    bias = jnp.where(core == 0, bias_ref[:, :BLK], bias_ref[:, BLK:])
    blended = jnp.concatenate(parts, axis=0).T + bias
    result = jnp.where(blended > 0, blended, jnp.exp(jnp.minimum(blended, 0.0)) - 1.0).astype(jnp.bfloat16)
    half_ref[...] = jnp.where(core == 0, result[OWN:], result[:OWN])
    result_pair().start()
    kept_half[...] = jnp.where(core == 0, result[:OWN], result[OWN:])
    keep = pltpu.make_async_copy(kept_half, out_ref.at[:, pl.ds(pl.multiple_of(core * BLK, BLK), BLK)], local.at[10])
    keep.start()

    for d in range(1, ZS):
        stats_z(d).wait_send()
        sums_z(d).wait_send()
    keep.wait()
    result_pair().wait()


def layer(source, target, weight, score_source, score_target, bias, slots, live, bits):
    dma = pltpu.SemaphoreType.DMA
    vmem = pltpu.VMEM
    f32, bf16 = jnp.float32, jnp.bfloat16
    return pl.pallas_call(
        layer_kernel,
        out_shape=pltpu.VMEM((OWN, WIDTH), bf16),
        in_specs=[pl.BlockSpec(memory_space=pltpu.HBM)] * 9,
        out_specs=pl.BlockSpec(memory_space=pltpu.VMEM),
        scratch_shapes=[
            vmem((OWN, WIDTH), bf16),
            vmem((OWN, WIDTH), bf16),
            vmem((WIDTH, WIDTH), bf16),
            vmem((HEADS, HD), f32),
            vmem((HEADS, HD), f32),
            vmem((1, WIDTH), f32),
            pltpu.SMEM((1, SLOTS), jnp.int32),
            pltpu.SMEM((1, 1), jnp.int32),
            vmem((SLOTS, BLK // 8, BLK), jnp.int32),
            vmem((ROWS, OWN, WIDTH), bf16),
            vmem((XS, YS, HEADS, BLK), f32),
            vmem((2, HEADS, BLK), f32),
            vmem((DB, HEADS, BLK), f32),
            vmem((1, BLK), jnp.int32),
            pltpu.SMEM((1, BLK), jnp.int32),
            vmem((BLK, BLK), f32),
            vmem((HEADS, SB, BLK, BLK), f32),
            vmem((SLOTS + 1, HEADS, 8, BLK), f32),
            vmem((DB, HEADS, BLK), f32),
            vmem((SB, WIDTH, BLK), bf16),
            vmem((SLOTS, HEADS, BLK, BLK), bf16),
            vmem((SLOTS + 1, HEADS, 8, BLK), f32),
            vmem((SLOTS + 1, WIDTH, BLK), f32),
            vmem((DB, WIDTH, BLK), f32),
            vmem((DB, WIDTH, BLK), bf16),
            vmem((DB, 8, BLK), f32),
            vmem((DB, BLK, BLK), bf16),
            vmem((DB, 8, BLK), f32),
            vmem((DB, BLK, BLK), bf16),
            vmem((DB, 8, BLK), f32),
            vmem((DB, BLK, BLK), bf16),
            vmem((DB, 8, BLK), f32),
            vmem((OWN, BLK), bf16),
            vmem((OWN, BLK), bf16),
            dma((11,)),
            dma((YS,)), dma((YS,)),
            dma((XS,)), dma((XS,)),
            dma((ZS,)), dma((ZS,)),
            dma((YS,)), dma((YS,)),
            dma((YS, XS)), dma((YS, XS)),
            dma((ZS,)), dma((ZS,)),
            dma((ZS,)), dma((ZS,)),
            dma((ZS,)), dma((ZS,)),
            dma((3,)), dma((3,)),
        ],
        compiler_params=pltpu.CompilerParams(collective_id=0, has_side_effects=True, vmem_limit_bytes=60 << 20),
        name="layer",
    )(source, target, weight, score_source, score_target, bias, slots, live, bits)


def body(
    source_features, target_features, weight, score_source, score_target, out_bias,
    block_list, block_count, edge_bits,
):
    return layer(
        source_features[0], target_features, weight, score_source, score_target, out_bias.reshape(1, WIDTH),
        block_list[0], block_count, edge_bits[0, 0],
    )


def solution(mesh):
    placed = (
        P("col", "row", None),
        P(("row", "col"), None),
        P(),
        P(),
        P(),
        P(),
        P("row", "col", None),
        P("row", "col"),
        P("row", "col", None, None, None),
    )
    return jax.shard_map(
        body, mesh=mesh, in_specs=placed, out_specs=P(("row", "col"), None), check_vma=False
    )
```
